128 devices in a mesh: row: 64 (over x, z, y), col: 2 (over core).
Axes of the slice: x: 4, y: 4, z: 4, core: 2. Of those that a mesh axis runs over, the one named last changes fastest.
Arguments:
- blocks: float32 [1024, 25, 128, 128], P('row'), may hold values from -1 to 1, as said below
- columns: int32 [1024, 25], P('row'), may hold values from 0 to 1023, as said below
- current: float32 [64, 131072], P('col', 'row'), may hold values from -90 to 90
- directions: float32 [64, 131072], P('col', 'row'), may hold values from -90 to 90
- ritz_values: float32 [64], P('col'), may hold values from -1.5 to 1.5
- rotation: float32 [192, 64], replicated, may hold values from -0.4375 to 0.4375
Outputs:
- next_current: float32 [64, 131072], P('col', 'row')
- next_directions: float32 [64, 131072], P('col', 'row')
- projected: float32 [64, 64], replicated
The draws below stay inside these ranges and needn't reach their ends.
Inputs may be any that keep to these rules, and one draw needn't show every extreme that they name: Slot 0 of block row i holds column i. Its other slots hold distinct columns (i + d) mod 1024 with 1 <= d <= 32, and d = 32 occurs in every block row. `blocks`: slot 0 of every block row is a symmetric block.
All inputs are finite; a program needn't handle non-finite values.
Results may differ from the reference program's by a relative error of at most 0.0003.
Values sent between devices are 32-bit elements; how exact they have to be, the bound alone decides.
A program may use at most 128 MiB of HBM per device.

```python
import math
import jax
import jax.numpy as jnp
from jax import lax

BLOCK = 128
NV = 64
SLOTS = 25
WB = 32
NBLK = 1024
NTOT = 131072


def draw_blocks(key, part):
    key = jax.random.fold_in(key, 11)
    raw = jnp.clip(jax.random.normal(key, (NBLK, SLOTS, BLOCK, BLOCK), jnp.float32), -5.0, 5.0)
    middle = (raw[:, 0] + jnp.swapaxes(raw[:, 0], 1, 2)) * 0.7071
    raw = raw.at[:, 0].set(middle)
    return raw * (1.0 / math.sqrt(2 * SLOTS * BLOCK))


def draw_columns(key, part):
    key = jax.random.fold_in(key, 23)
    first_key, second_key = jax.random.split(key)
    scores = jax.random.randint(first_key, (NBLK, WB - 1), 0, 4096) * (WB - 1) + jnp.arange(WB - 1, dtype=jnp.int32)
    order = jnp.argsort(scores, axis=1).astype(jnp.int32)
    offsets = jnp.concatenate([jnp.full((NBLK, 1), WB, jnp.int32), order[:, :SLOTS - 2] + 1], axis=1)
    mixing = jax.random.randint(second_key, (NBLK, SLOTS - 1), 0, 4096) * (SLOTS - 1) + jnp.arange(SLOTS - 1, dtype=jnp.int32)
    shuffle = jnp.argsort(mixing, axis=1).astype(jnp.int32)
    offsets = jnp.take_along_axis(offsets, shuffle, axis=1)
    rows = jnp.arange(NBLK, dtype=jnp.int32)[:, None]
    tail = jnp.mod(rows + offsets, NBLK)
    return jnp.concatenate([rows, tail], axis=1).astype(jnp.int32)


def tilted_rows(key, noise, shared_weight):
    scale_key, shared_key, weight_key = jax.random.split(key, 3)
    places = jnp.arange(NTOT, dtype=jnp.float32) / NTOT
    rough = jax.random.uniform(scale_key, (NTOT,), jnp.float32)
    scales = jnp.exp(math.log(3.0) * places + math.log(3.3) * rough)
    shared = jnp.clip(jax.random.normal(shared_key, (NTOT,), jnp.float32), -4.0, 4.0)
    weights = jnp.clip(jax.random.normal(weight_key, (NV, 1), jnp.float32), -3.0, 3.0)
    return 0.5 * scales[None, :] * (noise + shared_weight * weights * shared[None, :])


def draw_current(key, part):
    key = jax.random.fold_in(key, 37)
    noise_key, rest_key = jax.random.split(key)
    noise = jnp.clip(jax.random.normal(noise_key, (NV, NTOT), jnp.float32), -4.0, 4.0)
    return tilted_rows(rest_key, noise, 0.6)


def draw_directions(key, part):
    key = jax.random.fold_in(key, 53)
    noise_key, rest_key = jax.random.split(key)
    noise = jnp.clip(jax.random.normal(noise_key, (NV, NTOT), jnp.float32), -4.0, 4.0)
    return tilted_rows(rest_key, noise, 0.6)


def shard_levels(key, dims, cuts, low, largest):
    factor_of = 1.0
    for dim, shards_of in cuts:
        steps = jax.random.uniform(jax.random.fold_in(jax.random.fold_in(key, 6), dim), (shards_of,), jnp.float32, low / len(cuts), largest / len(cuts))
        factor_of = factor_of * jnp.repeat(jnp.exp(steps), dims[dim] // shards_of).reshape((-1,) + (1,) * (len(dims) - 1 - dim))
    return factor_of


def bell_draw(own_key, dims, width, bound, kind=jnp.bfloat16):
    return jnp.clip(width * jax.random.normal(own_key, dims, jnp.float32), -bound, bound).astype(kind)


def setup_inputs(seed: int = 0) -> dict:
    streams_of = jax.random.split(jax.random.key(seed), 7)
    return {
        "blocks": draw_blocks(jax.random.fold_in(streams_of[6], 71), 0),
        "columns": draw_columns(jax.random.fold_in(streams_of[6], 71), 0),
        "current": draw_current(jax.random.fold_in(streams_of[6], 71), 0),
        "directions": draw_directions(jax.random.fold_in(streams_of[6], 71), 0),
        "ritz_values": jnp.clip(jax.random.uniform(streams_of[4], (NV,), jnp.float32, -1.5, 1.5) * shard_levels(streams_of[4], (NV,), ((0, 2),), -0.4, 0.0), -1.5, 1.5),
        "rotation": bell_draw(streams_of[5], (3 * NV, NV), (3 * NV) ** -0.5, 0.4375, jnp.float32),
    }


HIGH = lax.Precision.HIGHEST

def apply_h(blocks, columns, vectors):
    count = vectors.shape[0]
    grid = vectors.reshape(count, NBLK, BLOCK)

    def step(acc, inputs):
        block_row, column_row, index = inputs
        picked = grid[:, column_row, :]
        direct = jnp.einsum('sab,csb->ca', block_row, picked, precision=HIGH)
        mine = grid[:, index, :]
        back = jnp.einsum('sab,ca->csb', block_row[1:], mine, precision=HIGH)
        acc = acc.at[:, index, :].add(direct)
        acc = acc.at[:, column_row[1:], :].add(back)
        return (acc, None)
    start = jnp.zeros((count, NBLK, BLOCK), jnp.float32)
    result, unused = lax.scan(step, start, (blocks, columns, jnp.arange(NBLK, dtype=jnp.int32)))
    return result.reshape(count, NBLK * BLOCK)

def reference(blocks, columns, current, directions, ritz_values, rotation):
    hx = apply_h(blocks, columns, current)
    hp = apply_h(blocks, columns, directions)
    resid = hx - ritz_values[:, None] * current
    hr = apply_h(blocks, columns, resid)
    basis = jnp.concatenate([current, resid, directions], axis=0)
    image = jnp.concatenate([hx, hr, hp], axis=0)
    gram = jnp.dot(basis, basis.T, precision=HIGH) / NTOT
    kmat = jnp.dot(basis, image.T, precision=HIGH) / NTOT
    small = jnp.dot(jnp.dot(rotation.T, gram, precision=HIGH), rotation, precision=HIGH)
    lower = jnp.linalg.cholesky(small)
    left = lax.linalg.triangular_solve(lower, rotation.T, left_side=True, lower=True)
    next_current = jnp.dot(left, basis, precision=HIGH)
    next_directions = jnp.dot(left[:, NV:], basis[NV:], precision=HIGH)
    projected = jnp.dot(jnp.dot(left, kmat, precision=HIGH), left.T, precision=HIGH)
    return (next_current, next_directions, projected)
```

```python
import functools

import jax
import jax.numpy as jnp
from jax import lax
from jax.experimental import pallas as pl
from jax.experimental.pallas import tpu as pltpu
from jax.sharding import PartitionSpec as P

WB = 32
F32 = jnp.float32
BF16 = jnp.bfloat16
MESH = pl.DeviceIdType.MESH
NN = (((1,), (0,)), ((), ()))
NT = (((1,), (1,)), ((), ()))
TN = (((0,), (0,)), ((), ()))
HIGH = lax.Precision.HIGHEST

RB = 8
W = 128
L = RB * W
SLABS = WB // RB + 1
CH = 256


def mm(a, b, dims):
    return lax.dot_general(a, b, dims, preferred_element_type=F32)


def mm_high(a, b, dims):
    return lax.dot_general(a, b, dims, precision=HIGH, preferred_element_type=F32)


def split(v):
    hi = v.astype(BF16)
    return hi, (v - hi.astype(F32)).astype(BF16)


def inverse_factor(g):
    n = g.shape[0]
    rows = lax.broadcasted_iota(jnp.int32, (n, 2 * n), 0)
    lanes = lax.broadcasted_iota(jnp.int32, (n, 2 * n), 1)
    eye = jnp.where(rows + n == lanes, 1.0, 0.0).astype(F32)
    a = jnp.concatenate([g, jnp.zeros((n, n), F32)], axis=1) + eye

    def step(k, a):
        row = jnp.sum(jnp.where(rows == k, a, 0.0), axis=0, keepdims=True)
        col = jnp.sum(jnp.where(lanes == k, a, 0.0), axis=1, keepdims=True)
        pivot = jnp.sum(jnp.where(lanes[:1] == k, row, 0.0), axis=1, keepdims=True)
        factor = jnp.where(rows[:, :1] > k, col / pivot, 0.0)
        return a - factor * row

    a = lax.fori_loop(0, n, step, a)
    diag = jnp.sum(jnp.where(rows == lanes, a, 0.0), axis=1, keepdims=True)
    return a[:, n:] * (1.0 / jnp.sqrt(diag))


def kernel(dims, ntot, inv_ref, blocks, current, directions, ritz, rot, nc, nd, proj, *scratch):
    stages = scratch[:RB]
    (mh, ml, xw, xx, zw, zz, pbuf, inbuf, tb, hx, pv, lam, ostage, arbuf,
     blk_sem, loc_sem, exs, exr, xs, xr, zs, zr, bs, br, ars, arr, outs, outr) = scratch[RB:]
    half, full = current.shape
    slots = blocks.shape[1]
    rows_n = 1
    for m in dims:
        rows_n *= m
    units = 2 * rows_n
    r = lax.axis_index("row")
    h = lax.axis_index("col")
    u = 2 * r + h
    down = lax.rem(u + units - 1, units)
    up = lax.rem(u + 1, units)
    down_id = (down // 2, lax.rem(down, 2))
    up_id = (up // 2, lax.rem(up, 2))
    sib = (r, 1 - h)

    groups = [(2, h, lambda c: (r, c))]
    stride = 1
    for m in reversed(dims):
        c = lax.rem(r // stride, m)
        groups.append((m, c, functools.partial(lambda c, stride, k: (r + (k - c) * stride, h), c, stride)))
        stride *= m

    for i in range(RB):
        pltpu.make_async_copy(
            blocks.at[h * RB + i], stages[i].at[pl.ds(0, slots)], blk_sem.at[i]
        ).start()
    mine = pl.multiple_of(h * L, L)
    other = pl.multiple_of((1 - h) * L, L)
    hrows = pl.multiple_of(h * half, half)
    loc_x = pltpu.make_async_copy(current.at[:, pl.ds(mine, L)], xw.at[0, pl.ds(hrows, half)], loc_sem.at[0])
    loc_x.start()
    loc_p = pltpu.make_async_copy(directions.at[:, pl.ds(mine, L)], pv.at[pl.ds(hrows, half)], loc_sem.at[1])
    loc_p.start()

    barrier = pltpu.get_barrier_semaphore()
    partners = [down_id, up_id]
    for m, c, member in groups:
        for k in range(1, m):
            partners.append(member(lax.rem(c + k, m)))
    for d in partners:
        pl.semaphore_signal(barrier, inc=1, device_id=d, device_id_type=MESH)

    er = lax.broadcasted_iota(jnp.int32, (half, half), 0) == lax.broadcasted_iota(jnp.int32, (half, half), 1)
    lam_own = jnp.sum(jnp.where(er, jnp.broadcast_to(ritz[...], (half, half)), 0.0), axis=1, keepdims=True)
    lam[pl.ds(hrows, half), :] = jnp.broadcast_to(lam_own, (half, W))
    for i in range(RB):
        stages[i][slots] = jnp.zeros((W, W), F32)
    zero = jnp.zeros((W, W), BF16)
    for j in range(0, RB, 2):
        for m_ref in (mh, ml):
            m_ref[(j + 1) * W:(j + 2) * W, j * W:(j + 1) * W] = zero
            m_ref[j * W:(j + 1) * W, (WB + j + 1) * W:(WB + j + 2) * W] = zero
    pl.semaphore_wait(barrier, len(partners))

    def remote(src, dst, ssem, rsem, dev):
        return pltpu.make_async_remote_copy(
            src_ref=src, dst_ref=dst, send_sem=ssem, recv_sem=rsem, device_id=dev, device_id_type=MESH)

    ex = [
        remote(current.at[:, pl.ds(other, L)], xw.at[0, pl.ds(hrows, half)], exs.at[0], exr.at[0], sib),
        remote(directions.at[:, pl.ds(other, L)], pv.at[pl.ds(hrows, half)], exs.at[1], exr.at[1], sib),
        remote(lam.at[pl.ds(hrows, half)], lam.at[pl.ds(hrows, half)], exs.at[2], exr.at[2], sib),
    ]
    for c in ex:
        c.start()
    xcopy = [remote(xw.at[t], xw.at[t + 1], xs.at[t], xr.at[t], down_id) for t in range(SLABS - 1)]
    zcopy = [remote(zw.at[t], zw.at[t + 1], zs.at[t], zr.at[t], down_id) for t in range(SLABS - 1)]
    bcopy = [remote(pbuf.at[t], inbuf.at[t], bs.at[t], br.at[t], up_id) for t in range(SLABS - 1)]

    def to_parts(t):
        hi, lo = split(xw[t])
        xx[t, :2 * half] = hi
        xx[t, 2 * half:] = lo

    def expand(i):
        pltpu.make_async_copy(
            blocks.at[h * RB + i], stages[i].at[pl.ds(0, slots)], blk_sem.at[i]
        ).wait()
        hi, lo = split(stages[i][0] * 0.5)
        mh[i * W:(i + 1) * W, i * W:(i + 1) * W] = hi
        ml[i * W:(i + 1) * W, i * W:(i + 1) * W] = lo

        def one(d, carry):
            hi, lo = split(stages[i][inv_ref[h * RB + i, d]])
            at = pl.multiple_of((i + d) * W, W)
            mh[i * W:(i + 1) * W, pl.ds(at, W)] = hi
            ml[i * W:(i + 1) * W, pl.ds(at, W)] = lo
            return carry

        lax.fori_loop(1, WB + 1, one, 0, unroll=4)

    def times_m(src, t, write):
        def chunk(j, lo, hi):
            at = pl.multiple_of(t * L + j * CH, CH)
            a = mm(src[:, lo:hi], mh[lo:hi, pl.ds(at, CH)], NN)
            b = mm(src[:2 * half, lo:hi], ml[lo:hi, pl.ds(at, CH)], NN)
            write(pl.ds(pl.multiple_of(j * CH, CH), CH), a[:2 * half] + a[2 * half:] + b)

        if t == 0 or t == SLABS - 1:
            for j in range(L // CH):
                chunk(j, *((0, (j + 1) * CH) if t == 0 else (j * CH, L)))
        else:
            def body(j, carry):
                chunk(j, 0, L)
                return carry
            lax.fori_loop(0, L // CH, body, 0)

    def times_mt(t):
        def chunk(j, lo, hi):
            at = pl.ds(pl.multiple_of(j * CH, CH), CH)
            a = mm(xx[t, :, lo:hi], mh[at, t * L + lo:t * L + hi], NT)
            b = mm(xx[t, :2 * half, lo:hi], ml[at, t * L + lo:t * L + hi], NT)
            hx[:, at] += a[:2 * half] + a[2 * half:] + b

        if t == 0 or t == SLABS - 1:
            for j in range(L // CH):
                chunk(j, *((j * CH, L) if t == 0 else (0, (j + 1) * CH)))
        else:
            def body(j, carry):
                chunk(j, 0, L)
                return carry
            lax.fori_loop(0, L // CH, body, 0)

    def back(t):
        s = SLABS - 1 - t
        def put(at, v):
            pbuf[s, :, at] = v
        times_m(xx.at[0], t, put)
        if s > 0:
            bcopy[s - 1].wait_recv()
            pbuf[s] += inbuf[s - 1]
        bcopy[s].start()

    loc_x.wait()
    ex[0].wait()
    xcopy[0].start()
    to_parts(0)
    for i in range(RB):
        expand(i)
        if i == RB // 2:
            xcopy[0].wait_recv()
            xcopy[1].start()
    back(4)
    xcopy[1].wait_recv()
    xcopy[2].start()
    back(3)
    xcopy[2].wait_recv()
    xcopy[3].start()
    back(2)
    back(1)

    def put_hx(at, v):
        hx[:, at] = v
    times_m(xx.at[0], 0, put_hx)
    times_mt(0)
    for t in range(1, SLABS):
        if t == SLABS - 1:
            xcopy[t - 1].wait_recv()
        to_parts(t)
        times_mt(t)
    loc_p.wait()
    ex[1].wait()
    ex[2].wait()
    bcopy[SLABS - 2].wait_recv()

    rot_x = rot[:2 * half]
    rot_r = rot[2 * half:4 * half]
    rot_p = rot[4 * half:]
    for j in range(L // CH):
        at = slice(j * CH, (j + 1) * CH)
        x = xw[0, :, at]
        res = hx[:, at] + inbuf[SLABS - 2, :, at] - jnp.concatenate([lam[...]] * (CH // W), axis=1) * x
        zp = mm_high(rot_r, res, TN) + mm_high(rot_p, pv[:, at], TN)
        z = zp + mm_high(rot_x, x, TN)
        ostage[1, :, at] = zp
        zw[0, :, at] = z
        hi, lo = split(z)
        zz[:2 * half, at] = hi
        zz[2 * half:, at] = lo
    zcopy[0].start()

    def sum_start(which, g, value):
        m, c, member = groups[g]
        buf = arbuf.at[which, g]
        buf[c] = value
        for k in range(1, m):
            remote(buf.at[c], buf.at[c], ars.at[which, g, k - 1], arr.at[which, g, k - 1],
                   member(lax.rem(c + k, m))).start()

    def sum_finish(which, g):
        m, c, member = groups[g]
        buf = arbuf.at[which, g]
        for k in range(1, m):
            remote(buf.at[c], buf.at[c], ars.at[which, g, k - 1], arr.at[which, g, k - 1],
                   member(lax.rem(c + k, m))).wait()
        total = buf[0]
        for k in range(1, m):
            total = total + buf[k]
        return total

    def z_times_m(t):
        def put(at, v):
            tb[t, :, at] = v
        times_m(zz, t, put)

    def z_next(t):
        zcopy[t].wait_recv()
        if t + 1 < SLABS - 1:
            zcopy[t + 1].start()

    def s_part(t):
        return mm_high(tb[t], zw[t], NT)

    def fold(v):
        return jnp.concatenate([v[:half], v[half:]], axis=1)

    def unfold(v):
        return jnp.concatenate([v[:, :2 * half], v[:, 2 * half:]], axis=0)

    sum_start(0, 0, fold(mm_high(zw[0], zw[0], NT)))
    z_times_m(0)
    sum_start(0, 1, sum_finish(0, 0))
    z_next(0)
    z_times_m(1)
    sum_start(0, 2, sum_finish(0, 1))
    z_next(1)
    z_times_m(2)
    sum_start(0, 3, sum_finish(0, 2))
    z_times_m(3)
    z_next(2)
    small = unfold(sum_finish(0, 3)) * (1.0 / ntot)
    li = inverse_factor(small)
    z_times_m(4)
    for j in range(L // CH):
        at = slice(j * CH, (j + 1) * CH)
        ostage[0, :, at] = mm_high(li, zw[0, :, at], NN)
        ostage[1, :, at] = mm_high(li, ostage[1, :, at], NN)
    orows = pl.multiple_of((1 - h) * half, half)
    ocopy = []
    for k, out in enumerate((nc, nd)):
        ocopy.append(remote(ostage.at[k, pl.ds(orows, half)], out.at[:, pl.ds(mine, L)], outs.at[k], outr.at[k], sib))
        ocopy.append(pltpu.make_async_copy(ostage.at[k, pl.ds(hrows, half)], out.at[:, pl.ds(mine, L)], loc_sem.at[2 + k]))
    for c in ocopy:
        c.start()
    s = s_part(0)
    for t in range(1, SLABS - 1):
        s = s + s_part(t)
    z_next(SLABS - 2)
    s = s + s_part(SLABS - 1)
    sum_start(1, 0, fold(s))
    for g in range(1, len(groups)):
        sum_start(1, g, sum_finish(1, g - 1))
    s = unfold(sum_finish(1, len(groups) - 1)) * (1.0 / ntot)
    sym = s + jnp.transpose(s)
    proj[...] = mm_high(mm_high(li, sym, NN), li, NT)
    for c in ocopy:
        c.wait()
    for c in xcopy + zcopy + bcopy:
        c.wait_send()


def on_device(dims, ntot, blocks, columns, current, directions, ritz_values, rotation):
    rows_here, slots = columns.shape
    half, length = current.shape
    states = rotation.shape[1]
    total_rows = ntot // W
    rows = lax.axis_index("row") * rows_here + jnp.arange(rows_here, dtype=jnp.int32)
    offsets = jnp.mod(columns - rows[:, None], total_rows)
    hit = offsets[:, None, :] == jnp.arange(WB + 1, dtype=jnp.int32)[None, :, None]
    inv = slots + jnp.sum(jnp.where(hit, jnp.arange(slots, dtype=jnp.int32) - slots, 0), axis=2)

    any_ = pl.BlockSpec(memory_space=pl.ANY)
    vmem = pl.BlockSpec(memory_space=pltpu.VMEM)
    smem = pl.BlockSpec(memory_space=pltpu.SMEM)
    n_groups = 1 + len(dims)
    most = max((2,) + tuple(dims))
    dma = pltpu.SemaphoreType.DMA
    hops = SLABS - 1
    scratch = [pltpu.VMEM((slots + 1, W, W), F32) for _ in range(RB)] + [
        pltpu.VMEM((L, SLABS * L), BF16),
        pltpu.VMEM((L, SLABS * L), BF16),
        pltpu.VMEM((SLABS, states, L), F32),
        pltpu.VMEM((SLABS, 2 * states, L), BF16),
        pltpu.VMEM((SLABS, states, L), F32),
        pltpu.VMEM((2 * states, L), BF16),
        pltpu.VMEM((hops, states, L), F32),
        pltpu.VMEM((hops, states, L), F32),
        pltpu.VMEM((SLABS, states, L), F32),
        pltpu.VMEM((states, L), F32),
        pltpu.VMEM((states, L), F32),
        pltpu.VMEM((states, W), F32),
        pltpu.VMEM((2, states, L), F32),
        pltpu.VMEM((2, n_groups, most, half, 2 * states), F32),
        dma((RB,)), dma((4,)), dma((3,)), dma((3,)),
        dma((hops,)), dma((hops,)), dma((hops,)), dma((hops,)), dma((hops,)), dma((hops,)),
        dma((2, n_groups, most)), dma((2, n_groups, most)), dma((2,)), dma((2,)),
    ]
    return pl.pallas_call(
        functools.partial(kernel, dims, ntot),
        out_shape=(
            jax.ShapeDtypeStruct((half, length), F32),
            jax.ShapeDtypeStruct((half, length), F32),
            jax.ShapeDtypeStruct((states, states), F32),
        ),
        in_specs=[smem, any_, any_, any_, vmem, vmem],
        out_specs=(any_, any_, vmem),
        scratch_shapes=scratch,
        compiler_params=pltpu.CompilerParams(
            collective_id=0, has_side_effects=True, vmem_limit_bytes=58 * 2**20
        ),
        name="lobpcg",
    )(inv, blocks, current, directions, ritz_values.reshape(1, half), rotation)


def solution(mesh):
    rows_n = mesh.shape["row"]
    side = round(rows_n ** (1 / 3))
    dims = (side, side, rows_n // (side * side))
    in_specs = (
        P("row", None, None, None),
        P("row", None),
        P("col", "row"),
        P("col", "row"),
        P("col"),
        P(),
    )
    out_specs = (P("col", "row"), P("col", "row"), P())
    ntot = rows_n * 2 * L
    return jax.shard_map(
        functools.partial(on_device, dims, ntot), mesh=mesh, in_specs=in_specs, out_specs=out_specs, check_vma=False
    )
```

```python
import functools

import jax
import jax.numpy as jnp
from jax import lax
from jax.experimental import pallas as pl
from jax.experimental.pallas import tpu as pltpu
from jax.sharding import PartitionSpec as P

WB = 32
F32 = jnp.float32
BF16 = jnp.bfloat16
MESH = pl.DeviceIdType.MESH
NN = (((1,), (0,)), ((), ()))
NT = (((1,), (1,)), ((), ()))
TN = (((0,), (0,)), ((), ()))
HIGH = lax.Precision.HIGHEST

RB = 8
W = 128
L = RB * W
SLABS = WB // RB + 1
CH = 256


def mm(a, b, dims):
    return lax.dot_general(a, b, dims, preferred_element_type=F32)


def mm_high(a, b, dims):
    return lax.dot_general(a, b, dims, precision=HIGH, preferred_element_type=F32)


def split(v):
    hi = v.astype(BF16)
    return hi, (v - hi.astype(F32)).astype(BF16)


def inverse_factor(g):
    n = g.shape[0]
    rows = lax.broadcasted_iota(jnp.int32, (n, 2 * n), 0)
    lanes = lax.broadcasted_iota(jnp.int32, (n, 2 * n), 1)
    eye = jnp.where(rows + n == lanes, 1.0, 0.0).astype(F32)
    a = jnp.concatenate([g, jnp.zeros((n, n), F32)], axis=1) + eye

    def step(k, a):
        row = jnp.sum(jnp.where(rows == k, a, 0.0), axis=0, keepdims=True)
        col = jnp.sum(jnp.where(lanes == k, a, 0.0), axis=1, keepdims=True)
        pivot = jnp.sum(jnp.where(lanes[:1] == k, row, 0.0), axis=1, keepdims=True)
        factor = jnp.where(rows[:, :1] > k, col / pivot, 0.0)
        return a - factor * row

    a = lax.fori_loop(0, n, step, a)
    diag = jnp.sum(jnp.where(rows == lanes, a, 0.0), axis=1, keepdims=True)
    return a[:, n:] * (1.0 / jnp.sqrt(diag))


def kernel(dims, ntot, inv_ref, blocks, current, directions, ritz, rot, nc, nd, proj, *scratch):
    stages = scratch[:RB]
    (mh, ml, xw, xx, zw, zz, zzp, pbuf, inbuf, tb, tin, hx, pv, lam, rotv, ritzv, ostage, bufa, bufb,
     blk_sem, loc_sem, exs, exr, xs, xr, zs, zr, ts, tr, bs, br, asa, ara, asb, arb, outs, outr) = scratch[RB:]
    half, full = current.shape
    slots = blocks.shape[1]
    rows_n = 1
    for m in dims:
        rows_n *= m
    units = 2 * rows_n
    r = lax.axis_index("row")
    h = lax.axis_index("col")
    u = 2 * r + h
    down = lax.rem(u + units - 1, units)
    up = lax.rem(u + 1, units)
    down_id = (down // 2, lax.rem(down, 2))
    up_id = (up // 2, lax.rem(up, 2))
    sib = (r, 1 - h)

    ny = dims[-1]
    nb = rows_n // ny
    y = lax.rem(r, ny)
    groups = [
        (2 * ny, 2 * y + h, lambda k: (r - y + k // 2, lax.rem(k, 2)), (bufa, asa, ara)),
        (nb, r // ny, lambda k: (k * ny + y, h), (bufb, asb, arb)),
    ]

    def row_at(k):
        return (lax.rem(r + k + rows_n, rows_n), h)

    for i in range(RB):
        pltpu.make_async_copy(
            blocks.at[h * RB + i], stages[i].at[pl.ds(0, slots)], blk_sem.at[i]
        ).start()
    mine = pl.multiple_of(h * L, L)
    other = pl.multiple_of((1 - h) * L, L)
    hrows = pl.multiple_of(h * half, half)
    loc_x = pltpu.make_async_copy(current.at[:, pl.ds(mine, L)], xw.at[0, pl.ds(hrows, half)], loc_sem.at[0])
    loc_x.start()
    loc_p = pltpu.make_async_copy(directions.at[:, pl.ds(mine, L)], pv.at[pl.ds(hrows, half)], loc_sem.at[1])
    loc_p.start()
    loc_rot = pltpu.make_async_copy(rot, rotv, loc_sem.at[4])
    loc_rot.start()
    loc_ritz = pltpu.make_async_copy(ritz, ritzv, loc_sem.at[5])
    loc_ritz.start()

    barrier = pltpu.get_barrier_semaphore()
    partners = [down_id, up_id] + [row_at(k) for k in (-2, -1, 1, 2)]
    for m, c, member, _ in groups:
        for k in range(1, m):
            partners.append(member(lax.rem(c + k, m)))
    for d in partners:
        pl.semaphore_signal(barrier, inc=1, device_id=d, device_id_type=MESH)

    er = lax.broadcasted_iota(jnp.int32, (half, half), 0) == lax.broadcasted_iota(jnp.int32, (half, half), 1)
    loc_ritz.wait()
    lam_own = jnp.sum(jnp.where(er, jnp.broadcast_to(ritzv[...], (half, half)), 0.0), axis=1, keepdims=True)
    lam[pl.ds(hrows, half), :] = jnp.broadcast_to(lam_own, (half, W))
    for i in range(RB):
        stages[i][slots] = jnp.zeros((W, W), F32)
    zero = jnp.zeros((W, W), BF16)
    for j in range(0, RB, 2):
        for m_ref in (mh, ml):
            m_ref[(j + 1) * W:(j + 2) * W, j * W:(j + 1) * W] = zero
            m_ref[j * W:(j + 1) * W, (WB + j + 1) * W:(WB + j + 2) * W] = zero
    pl.semaphore_wait(barrier, len(partners))

    def remote(src, dst, ssem, rsem, dev):
        return pltpu.make_async_remote_copy(
            src_ref=src, dst_ref=dst, send_sem=ssem, recv_sem=rsem, device_id=dev, device_id_type=MESH)

    ex = [
        remote(current.at[:, pl.ds(other, L)], xw.at[0, pl.ds(hrows, half)], exs.at[0], exr.at[0], sib),
        remote(directions.at[:, pl.ds(other, L)], pv.at[pl.ds(hrows, half)], exs.at[1], exr.at[1], sib),
        remote(lam.at[pl.ds(hrows, half)], lam.at[pl.ds(hrows, half)], exs.at[2], exr.at[2], sib),
    ]
    for c in ex:
        c.start()
    xcopy = [remote(xw.at[t], xw.at[t + 1], xs.at[t], xr.at[t], down_id) for t in range(SLABS - 1)]
    zcopy = [remote(zw.at[0], zw.at[k], zs.at[k - 1], zr.at[k - 1], row_at(-k)) for k in (1, 2)]
    tcopy = [remote(tb.at[t], tin.at[t // 2], ts.at[t // 2], tr.at[t // 2], sib) for t in (1, 3)]
    bcopy = [remote(pbuf.at[t], inbuf.at[t], bs.at[t], br.at[t], up_id) for t in range(SLABS - 1)]

    def to_parts(t):
        hi, lo = split(xw[t])
        xx[t, :2 * half] = hi
        xx[t, 2 * half:] = lo

    def expand(i):
        pltpu.make_async_copy(
            blocks.at[h * RB + i], stages[i].at[pl.ds(0, slots)], blk_sem.at[i]
        ).wait()
        hi, lo = split(stages[i][0] * 0.5)
        mh[i * W:(i + 1) * W, i * W:(i + 1) * W] = hi
        ml[i * W:(i + 1) * W, i * W:(i + 1) * W] = lo

        def one(d, carry):
            hi, lo = split(stages[i][inv_ref[h * RB + i, d]])
            at = pl.multiple_of((i + d) * W, W)
            mh[i * W:(i + 1) * W, pl.ds(at, W)] = hi
            ml[i * W:(i + 1) * W, pl.ds(at, W)] = lo
            return carry

        lax.fori_loop(1, WB + 1, one, 0, unroll=4)

    def times_m(src, t, write):
        def chunk(j, lo, hi):
            at = pl.multiple_of(t * L + j * CH, CH)
            a = mm(src[:, lo:hi], mh[lo:hi, pl.ds(at, CH)], NN)
            b = mm(src[:2 * half, lo:hi], ml[lo:hi, pl.ds(at, CH)], NN)
            write(pl.ds(pl.multiple_of(j * CH, CH), CH), a[:2 * half] + a[2 * half:] + b)

        if t == 0 or t == SLABS - 1:
            for j in range(L // CH):
                chunk(j, *((0, (j + 1) * CH) if t == 0 else (j * CH, L)))
        else:
            def body(j, carry):
                chunk(j, 0, L)
                return carry
            lax.fori_loop(0, L // CH, body, 0)

    def times_mt(t):
        def chunk(j, lo, hi):
            at = pl.ds(pl.multiple_of(j * CH, CH), CH)
            a = mm(xx[t, :, lo:hi], mh[at, t * L + lo:t * L + hi], NT)
            b = mm(xx[t, :2 * half, lo:hi], ml[at, t * L + lo:t * L + hi], NT)
            hx[:, at] += a[:2 * half] + a[2 * half:] + b

        if t == 0 or t == SLABS - 1:
            for j in range(L // CH):
                chunk(j, *((j * CH, L) if t == 0 else (0, (j + 1) * CH)))
        else:
            def body(j, carry):
                chunk(j, 0, L)
                return carry
            lax.fori_loop(0, L // CH, body, 0)

    def back(t):
        s = SLABS - 1 - t
        def put(at, v):
            pbuf[s, :, at] = v
        times_m(xx.at[0], t, put)
        if s > 0:
            bcopy[s - 1].wait_recv()
            pbuf[s] += inbuf[s - 1]
        bcopy[s].start()

    loc_x.wait()
    ex[0].wait()
    xcopy[0].start()
    to_parts(0)
    for i in range(RB):
        expand(i)
        if i == RB // 2:
            xcopy[0].wait_recv()
            xcopy[1].start()
    back(4)
    xcopy[1].wait_recv()
    xcopy[2].start()
    back(3)
    xcopy[2].wait_recv()
    xcopy[3].start()
    back(2)
    back(1)

    def put_hx(at, v):
        hx[:, at] = v
    times_m(xx.at[0], 0, put_hx)
    times_mt(0)
    for t in range(1, SLABS):
        if t == SLABS - 1:
            xcopy[t - 1].wait_recv()
        to_parts(t)
        times_mt(t)
    loc_p.wait()
    ex[1].wait()
    ex[2].wait()
    bcopy[SLABS - 2].wait_recv()

    loc_rot.wait()
    n = 2 * half
    ct_hi, ct_lo = split(jnp.concatenate(
        [rotv[...], jnp.where(lax.broadcasted_iota(jnp.int32, (n, 3 * n), 1) < n, 0.0, rotv[...])], axis=0))
    ct = jnp.concatenate([ct_hi, ct_lo], axis=0)
    for j in range(L // CH):
        at = slice(j * CH, (j + 1) * CH)
        x = xw[0, :, at]
        res = hx[:, at] + inbuf[SLABS - 2, :, at] - jnp.concatenate([lam[...]] * (CH // W), axis=1) * x
        r_hi, r_lo = split(res)
        p_hi, p_lo = split(pv[:, at])
        b_hi = jnp.concatenate([xx[0, :n, at], r_hi, p_hi], axis=0)
        b_lo = jnp.concatenate([xx[0, n:, at], r_lo, p_lo], axis=0)
        both = mm(ct, b_hi, NN)
        both = both[:2 * n] + both[2 * n:] + mm(ct_hi, b_lo, NN)
        zw[0, :, at] = both[:n]
        hi, lo = split(both[:n])
        zz[:n, at] = hi
        zz[n:, at] = lo
        hi, lo = split(both[n:])
        zzp[:n, at] = hi
        zzp[n:, at] = lo
    for c in zcopy:
        c.start()

    def sum_copies(which, g):
        m, c, member, (buf, ssem, rsem) = groups[g]
        return [
            remote(buf.at[which, c], buf.at[which, c], ssem.at[which, k - 1], rsem.at[which, k - 1],
                   member(lax.rem(c + k, m)))
            for k in range(1, m)
        ]

    def sum_start(which, g, value):
        m, c, member, (buf, ssem, rsem) = groups[g]
        buf[which, c] = value
        for copy in sum_copies(which, g):
            copy.start()

    def sum_finish(which, g):
        m, c, member, (buf, ssem, rsem) = groups[g]
        for copy in sum_copies(which, g):
            copy.wait()
        total = buf[which, 0]
        for k in range(1, m):
            total = total + buf[which, k]
        return total

    def z_times_m(t):
        def put(at, v):
            tb[t, :, at] = v
        times_m(zz, t, put)

    def quarters(v):
        return v[:n, :n] + v[:n, n:] + v[n:, :n] + v[n:, n:]

    def s_part(k):
        if k:
            zcopy[k - 1].wait_recv()
            hi, lo = split(zw[k])
            other_z = jnp.concatenate([hi, lo], axis=0)
        else:
            other_z = zz[...]
        hi, lo = split(tb[2 * k])
        return mm(jnp.concatenate([hi, lo], axis=0), other_z, NT)

    def fold(v):
        return jnp.concatenate([v[:half], v[half:]], axis=1)

    def unfold(v):
        return jnp.concatenate([v[:, :n], v[:, n:]], axis=0)

    sum_start(0, 0, fold(quarters(mm(zz[...], zz[...], NT))))
    z_times_m(1)
    tcopy[0].start()
    z_times_m(3)
    tcopy[1].start()
    z_times_m(0)
    sum_start(0, 1, sum_finish(0, 0))
    z_times_m(2)
    z_times_m(4)
    tcopy[0].wait_recv()
    tb[2 * (1 - h)] += tin[0]
    tcopy[1].wait_recv()
    tb[2 * (2 - h)] += tin[1]
    s = s_part(0)
    s = s + s_part(1)
    s = s + s_part(2)
    sum_start(1, 0, fold(quarters(s)))
    small = unfold(sum_finish(0, 1)) * (1.0 / ntot)
    li = inverse_factor(small)
    sum_start(1, 1, sum_finish(1, 0))
    li_hi, li_lo = split(li)
    ll = jnp.concatenate([jnp.concatenate([li_hi, li_hi], axis=1), jnp.concatenate([li_lo, li_lo], axis=1)], axis=0)
    for j in range(L // CH):
        at = slice(j * CH, (j + 1) * CH)
        for k, src in enumerate((zz, zzp)):
            v = mm(ll, src[:, at], NN)
            ostage[k, :, at] = v[:n] + v[n:]
    orows = pl.multiple_of((1 - h) * half, half)
    ocopy = []
    for k, out in enumerate((nc, nd)):
        ocopy.append(remote(ostage.at[k, pl.ds(orows, half)], out.at[:, pl.ds(mine, L)], outs.at[k], outr.at[k], sib))
        ocopy.append(pltpu.make_async_copy(ostage.at[k, pl.ds(hrows, half)], out.at[:, pl.ds(mine, L)], loc_sem.at[2 + k]))
    for c in ocopy:
        c.start()
    s = unfold(sum_finish(1, 1)) * (1.0 / ntot)
    sym = s + jnp.transpose(s)
    proj[...] = mm_high(mm_high(li, sym, NN), li, NT)
    for c in ocopy:
        c.wait()
    for c in xcopy + zcopy + bcopy + tcopy:
        c.wait_send()


def place(*refs):
    for k in range(3):
        refs[3 + k][...] = refs[k][...]


def on_device(dims, ntot, blocks, columns, current, directions, ritz_values, rotation):
    rows_here, slots = columns.shape
    half, length = current.shape
    states = rotation.shape[1]
    total_rows = ntot // W
    rows = lax.axis_index("row") * rows_here + jnp.arange(rows_here, dtype=jnp.int32)
    offsets = jnp.mod(columns - rows[:, None], total_rows)
    hit = offsets[:, None, :] == jnp.arange(WB + 1, dtype=jnp.int32)[None, :, None]
    inv = slots + jnp.sum(jnp.where(hit, jnp.arange(slots, dtype=jnp.int32) - slots, 0), axis=2)

    any_ = pl.BlockSpec(memory_space=pl.ANY)
    vmem = pl.BlockSpec(memory_space=pltpu.VMEM)
    smem = pl.BlockSpec(memory_space=pltpu.SMEM)
    ga = 2 * dims[-1]
    gb = total_rows // rows_here // dims[-1]
    dma = pltpu.SemaphoreType.DMA
    hops = SLABS - 1
    scratch = [pltpu.VMEM((slots + 1, W, W), F32) for _ in range(RB)] + [
        pltpu.VMEM((L, SLABS * L), BF16),
        pltpu.VMEM((L, SLABS * L), BF16),
        pltpu.VMEM((SLABS, states, L), F32),
        pltpu.VMEM((SLABS, 2 * states, L), BF16),
        pltpu.VMEM((3, states, L), F32),
        pltpu.VMEM((2 * states, L), BF16),
        pltpu.VMEM((2 * states, L), BF16),
        pltpu.VMEM((hops, states, L), F32),
        pltpu.VMEM((hops, states, L), F32),
        pltpu.VMEM((SLABS, states, L), F32),
        pltpu.VMEM((2, states, L), F32),
        pltpu.VMEM((states, L), F32),
        pltpu.VMEM((states, L), F32),
        pltpu.VMEM((states, W), F32),
        pltpu.VMEM((states, 3 * states), F32),
        pltpu.VMEM((1, half), F32),
        pltpu.VMEM((2, states, L), F32),
        pltpu.VMEM((2, ga, half, 2 * states), F32),
        pltpu.VMEM((2, gb, half, 2 * states), F32),
        dma((RB,)), dma((6,)), dma((3,)), dma((3,)),
        dma((hops,)), dma((hops,)), dma((2,)), dma((2,)), dma((2,)), dma((2,)), dma((hops,)), dma((hops,)),
        dma((2, ga)), dma((2, ga)), dma((2, gb)), dma((2, gb)), dma((2,)), dma((2,)),
    ]
    outs = pl.pallas_call(
        functools.partial(kernel, dims, ntot),
        out_shape=(
            jax.ShapeDtypeStruct((half, length), F32),
            jax.ShapeDtypeStruct((half, length), F32),
            jax.ShapeDtypeStruct((states, states), F32),
        ),
        in_specs=[smem, any_, any_, any_, any_, any_],
        out_specs=(any_, any_, vmem),
        scratch_shapes=scratch,
        compiler_params=pltpu.CompilerParams(
            collective_id=0, has_side_effects=True, vmem_limit_bytes=58 * 2**20
        ),
        name="lobpcg",
    )(inv, blocks, current, directions, ritz_values.reshape(1, half), rotation.T)
    return pl.pallas_call(
        place,
        out_shape=tuple(jax.ShapeDtypeStruct(o.shape, o.dtype) for o in outs),
        in_specs=[vmem] * 3,
        out_specs=(vmem,) * 3,
        name="place",
    )(*outs)


def solution(mesh):
    rows_n = mesh.shape["row"]
    side = round(rows_n ** (1 / 3))
    dims = (side, side, rows_n // (side * side))
    in_specs = (
        P("row", None, None, None),
        P("row", None),
        P("col", "row"),
        P("col", "row"),
        P("col"),
        P(),
    )
    out_specs = (P("col", "row"), P("col", "row"), P())
    ntot = rows_n * 2 * L
    return jax.shard_map(
        functools.partial(on_device, dims, ntot), mesh=mesh, in_specs=in_specs, out_specs=out_specs, check_vma=False
    )
```

```python
import functools

import jax
import jax.numpy as jnp
from jax import lax
from jax.experimental import pallas as pl
from jax.experimental.pallas import tpu as pltpu
from jax.sharding import PartitionSpec as P

WB = 32
F32 = jnp.float32
BF16 = jnp.bfloat16
MESH = pl.DeviceIdType.MESH
NN = (((1,), (0,)), ((), ()))
NT = (((1,), (1,)), ((), ()))
TN = (((0,), (0,)), ((), ()))
HIGH = lax.Precision.HIGHEST

RB = 8
W = 128
L = RB * W
SLABS = WB // RB + 1
CH = 256


def mm(a, b, dims):
    return lax.dot_general(a, b, dims, preferred_element_type=F32)


def mm_high(a, b, dims):
    return lax.dot_general(a, b, dims, precision=HIGH, preferred_element_type=F32)


def split(v):
    hi = v.astype(BF16)
    return hi, (v - hi.astype(F32)).astype(BF16)


def factor_start(g):
    n = g.shape[0]
    rows = lax.broadcasted_iota(jnp.int32, (n, 2 * n), 0)
    lanes = lax.broadcasted_iota(jnp.int32, (n, 2 * n), 1)
    a = jnp.concatenate([g, jnp.zeros((n, n), F32)], axis=1) + jnp.where(rows + n == lanes, 1.0, 0.0).astype(F32)
    return [a[8 * i:8 * i + 8] for i in range(n // 8)]


def factor_steps(a, first, last):
    a = list(a)
    sub = lax.broadcasted_iota(jnp.int32, (8, 1), 0)
    for k in range(first, last):
        b, s = divmod(k, 8)
        row = a[b][s:s + 1, :]
        scaled = row * (1.0 / row[:, k:k + 1])
        for i in range(b, len(a)):
            col = a[i][:, k:k + 1]
            if i == b:
                col = jnp.where(sub > s, col, 0.0)
            a[i] = a[i] - col * scaled
    return a


def factor_end(a):
    a = jnp.concatenate(a, axis=0)
    n = a.shape[0]
    rows = lax.broadcasted_iota(jnp.int32, (n, 2 * n), 0)
    lanes = lax.broadcasted_iota(jnp.int32, (n, 2 * n), 1)
    diag = jnp.sum(jnp.where(rows == lanes, a, 0.0), axis=1, keepdims=True)
    return a[:, n:] * (1.0 / jnp.sqrt(diag))


def kernel(dims, ntot, inv_ref, blocks, current, directions, ritz, rot, nc, nd, proj, *scratch):
    stages = scratch[:RB]
    (mh, ml, xw, xx, zw, zz, zzp, part, inbuf, tb, tin, hx, pv, lam, rotv, ritzv, ostage, bufa, bufb,
     blk_sem, loc_sem, exs, exr, xs, xr, cs, cr, zs, zr, ts, tr, bs, br, asa, ara, asb, arb, outs, outr) = scratch[RB:]
    half, full = current.shape
    slots = blocks.shape[1]
    rows_n = 1
    for m in dims:
        rows_n *= m
    r = lax.axis_index("row")
    h = lax.axis_index("col")
    sib = (r, 1 - h)

    ny = dims[-1]
    nb = rows_n // ny
    y = lax.rem(r, ny)
    groups = [
        (2 * ny, 2 * y + h, lambda k: (r - y + k // 2, lax.rem(k, 2)), (bufa, asa, ara)),
        (nb, r // ny, lambda k: (k * ny + y, h), (bufb, asb, arb)),
    ]

    def row_at(k):
        return (lax.rem(r + k + rows_n, rows_n), h)

    for i in range(RB):
        pltpu.make_async_copy(
            blocks.at[h * RB + i], stages[i].at[pl.ds(0, slots)], blk_sem.at[i]
        ).start()
    mine = pl.multiple_of(h * L, L)
    other = pl.multiple_of((1 - h) * L, L)
    hrows = pl.multiple_of(h * half, half)
    loc_x = pltpu.make_async_copy(current.at[:, pl.ds(mine, L)], xw.at[h, pl.ds(hrows, half)], loc_sem.at[0])
    loc_x.start()
    loc_p = pltpu.make_async_copy(directions.at[:, pl.ds(mine, L)], pv.at[pl.ds(hrows, half)], loc_sem.at[1])
    loc_p.start()
    loc_rot = pltpu.make_async_copy(rot, rotv, loc_sem.at[4])
    loc_rot.start()
    loc_ritz = pltpu.make_async_copy(ritz, ritzv, loc_sem.at[5])
    loc_ritz.start()

    barrier = pltpu.get_barrier_semaphore()
    partners = [row_at(k) for k in (-2, -1, 1, 2)]
    for m, c, member, _ in groups:
        for k in range(1, m):
            partners.append(member(lax.rem(c + k, m)))
    for d in partners:
        pl.semaphore_signal(barrier, inc=1, device_id=d, device_id_type=MESH)

    er = lax.broadcasted_iota(jnp.int32, (half, half), 0) == lax.broadcasted_iota(jnp.int32, (half, half), 1)
    loc_ritz.wait()
    lam_own = jnp.sum(jnp.where(er, jnp.broadcast_to(ritzv[...], (half, half)), 0.0), axis=1, keepdims=True)
    lam[pl.ds(hrows, half), :] = jnp.broadcast_to(lam_own, (half, W))
    for i in range(RB):
        stages[i][slots] = jnp.zeros((W, W), F32)
    zero = jnp.zeros((W, W), BF16)
    for j in range(0, RB, 2):
        for m_ref in (mh, ml):
            m_ref[(j + 1) * W:(j + 2) * W, j * W:(j + 1) * W] = zero
            m_ref[j * W:(j + 1) * W, (WB + j + 1) * W:(WB + j + 2) * W] = zero
    pl.semaphore_wait(barrier, len(partners))

    def remote(src, dst, ssem, rsem, dev):
        return pltpu.make_async_remote_copy(
            src_ref=src, dst_ref=dst, send_sem=ssem, recv_sem=rsem, device_id=dev, device_id_type=MESH)

    ex = [
        remote(current.at[:, pl.ds(other, L)], xw.at[1 - h, pl.ds(hrows, half)], exs.at[0], exr.at[0], sib),
        remote(directions.at[:, pl.ds(other, L)], pv.at[pl.ds(hrows, half)], exs.at[1], exr.at[1], sib),
        remote(lam.at[pl.ds(hrows, half)], lam.at[pl.ds(hrows, half)], exs.at[2], exr.at[2], sib),
    ]
    for c in ex:
        c.start()
    xcopy = [remote(xw.at[h], xw.at[h + 2 * k], xs.at[k - 1], xr.at[k - 1], row_at(-k)) for k in (1, 2)]
    shared = [remote(xw.at[w], xw.at[w], cs.at[k], cr.at[k], sib) for k, w in enumerate((1, 2 + h, 4))]
    got = remote(xw.at[3 - h], xw.at[3 - h], cs.at[1], cr.at[1], sib)
    zcopy = remote(zw.at[0], zw.at[1], zs, zr, row_at(-1))
    tcopy = [remote(tb.at[t], tin.at[k], ts.at[k], tr.at[k], dev) for k, (t, dev) in enumerate(((1, sib), (3, sib), (4, row_at(1))))]
    scopy = [remote(part.at[t], inbuf.at[t], bs.at[t], br.at[t], sib) for t in (1, 3)]
    bcopy = [remote(part.at[t], inbuf.at[t], bs.at[t], br.at[t], row_at(t // 2)) for t in (2, 4)]

    def to_parts(t):
        hi, lo = split(xw[h + t])
        xx[t, :2 * half] = hi
        xx[t, 2 * half:] = lo

    def expand(i):
        pltpu.make_async_copy(
            blocks.at[h * RB + i], stages[i].at[pl.ds(0, slots)], blk_sem.at[i]
        ).wait()
        hi, lo = split(stages[i][0] * 0.5)
        mh[i * W:(i + 1) * W, i * W:(i + 1) * W] = hi
        ml[i * W:(i + 1) * W, i * W:(i + 1) * W] = lo

        def one(d, carry):
            hi, lo = split(stages[i][inv_ref[h * RB + i, d]])
            at = pl.multiple_of((i + d) * W, W)
            mh[i * W:(i + 1) * W, pl.ds(at, W)] = hi
            ml[i * W:(i + 1) * W, pl.ds(at, W)] = lo
            return carry

        lax.fori_loop(1, WB + 1, one, 0, unroll=4)

    def times_m(src, t, write):
        def chunk(j, lo, hi):
            at = pl.multiple_of(t * L + j * CH, CH)
            a = mm(src[:, lo:hi], mh[lo:hi, pl.ds(at, CH)], NN)
            b = mm(src[:2 * half, lo:hi], ml[lo:hi, pl.ds(at, CH)], NN)
            write(pl.ds(pl.multiple_of(j * CH, CH), CH), a[:2 * half] + a[2 * half:] + b)

        if t == 0 or t == SLABS - 1:
            for j in range(L // CH):
                chunk(j, *((0, (j + 1) * CH) if t == 0 else (j * CH, L)))
        else:
            def body(j, carry):
                chunk(j, 0, L)
                return carry
            lax.fori_loop(0, L // CH, body, 0)

    def times_mt(t):
        def chunk(j, lo, hi):
            at = pl.ds(pl.multiple_of(j * CH, CH), CH)
            a = mm(xx[t, :, lo:hi], mh[at, t * L + lo:t * L + hi], NT)
            b = mm(xx[t, :2 * half, lo:hi], ml[at, t * L + lo:t * L + hi], NT)
            hx[:, at] += a[:2 * half] + a[2 * half:] + b

        if t == 0 or t == SLABS - 1:
            for j in range(L // CH):
                chunk(j, *((j * CH, L) if t == 0 else (0, (j + 1) * CH)))
        else:
            def body(j, carry):
                chunk(j, 0, L)
                return carry
            lax.fori_loop(0, L // CH, body, 0)

    def back(t):
        def put(at, v):
            part[t, :, at] = v
        times_m(xx.at[0], t, put)

    loc_x.wait()
    for i in range(RB // 2):
        expand(i)
    ex[0].wait()
    for c in xcopy:
        c.start()
    pl.when(h == 1)(shared[0].start)
    for i in range(RB // 2, RB):
        expand(i)
    to_parts(0)
    back(3)
    scopy[1].start()
    back(4)
    scopy[1].wait_recv()

    @pl.when(h == 0)
    def _():
        part[4] += inbuf[3]
    bcopy[1].start()
    back(1)
    scopy[0].start()
    back(2)
    scopy[0].wait_recv()
    part[2] += inbuf[3 - 2 * (1 - h)]
    bcopy[0].start()

    def put_hx(at, v):
        hx[:, at] = v
    times_m(xx.at[0], 0, put_hx)
    xcopy[0].wait_recv()
    shared[1].start()
    times_mt(0)
    pl.when(h == 0)(shared[0].wait_recv)
    pl.when(h == 1)(got.wait_recv)
    to_parts(1)
    times_mt(1)
    to_parts(2)
    times_mt(2)
    xcopy[1].wait_recv()
    pl.when(h == 0)(shared[2].start)
    to_parts(4)
    times_mt(4)
    pl.when(h == 0)(got.wait_recv)
    pl.when(h == 1)(shared[2].wait_recv)
    to_parts(3)
    times_mt(3)
    loc_p.wait()
    ex[1].wait()
    ex[2].wait()
    for c in bcopy:
        c.wait_recv()

    @pl.when(h == 1)
    def _():
        hx[...] += inbuf[1]

    loc_rot.wait()
    n = 2 * half
    ct_hi, ct_lo = split(jnp.concatenate(
        [rotv[...], jnp.where(lax.broadcasted_iota(jnp.int32, (n, 3 * n), 1) < n, 0.0, rotv[...])], axis=0))
    ct = jnp.concatenate([ct_hi, ct_lo], axis=0)
    for j in range(L // CH):
        at = slice(j * CH, (j + 1) * CH)
        x = xw[h, :, at]
        res = hx[:, at] + inbuf[2, :, at] + inbuf[4, :, at] - jnp.concatenate([lam[...]] * (CH // W), axis=1) * x
        r_hi, r_lo = split(res)
        p_hi, p_lo = split(pv[:, at])
        b_hi = jnp.concatenate([xx[0, :n, at], r_hi, p_hi], axis=0)
        b_lo = jnp.concatenate([xx[0, n:, at], r_lo, p_lo], axis=0)
        both = mm(ct, b_hi, NN)
        both = both[:2 * n] + both[2 * n:] + mm(ct_hi, b_lo, NN)
        zw[0, :, at] = both[:n]
        hi, lo = split(both[:n])
        zz[:n, at] = hi
        zz[n:, at] = lo
        hi, lo = split(both[n:])
        zzp[:n, at] = hi
        zzp[n:, at] = lo

    def sum_copies(which, g):
        m, c, member, (buf, ssem, rsem) = groups[g]
        return [
            remote(buf.at[which, c], buf.at[which, c], ssem.at[which, k - 1], rsem.at[which, k - 1],
                   member(lax.rem(c + k, m)))
            for k in range(1, m)
        ]

    def sum_start(which, g, value):
        m, c, member, (buf, ssem, rsem) = groups[g]
        buf[which, c] = value
        for copy in sum_copies(which, g):
            copy.start()

    def sum_finish(which, g):
        m, c, member, (buf, ssem, rsem) = groups[g]
        for copy in sum_copies(which, g):
            copy.wait()
        total = buf[which, 0]
        for k in range(1, m):
            total = total + buf[which, k]
        return total

    def z_times_m(t):
        def put(at, v):
            tb[t, :, at] = v
        times_m(zz, t, put)

    def quarters(v):
        return v[:n, :n] + v[:n, n:] + v[n:, :n] + v[n:, n:]

    def s_part(k):
        if k:
            hi, lo = split(zw[k])
            other_z = jnp.concatenate([hi, lo], axis=0)
        else:
            other_z = zz[...]
        hi, lo = split(tb[2 * k])
        return mm(jnp.concatenate([hi, lo], axis=0), other_z, NT)

    def fold(v):
        return jnp.concatenate([v[:half], v[half:]], axis=1)

    def unfold(v):
        return jnp.concatenate([v[:, :n], v[:, n:]], axis=0)

    sum_start(0, 0, fold(quarters(mm(zz[...], zz[...], NT))))
    zcopy.start()
    z_times_m(3)
    tcopy[1].start()
    z_times_m(4)
    tcopy[1].wait_recv()

    @pl.when(h == 0)
    def _():
        tb[4] += tin[1]
    tcopy[2].start()
    z_times_m(1)
    tcopy[0].start()
    sum_start(0, 1, sum_finish(0, 0))
    z_times_m(0)
    z_times_m(2)
    tcopy[0].wait_recv()
    tb[2 * (1 - h)] += tin[0]

    @pl.when(h == 1)
    def _():
        tb[2] += tin[1]
    s = s_part(0)
    zcopy.wait_recv()
    tcopy[2].wait_recv()
    tb[2] += tin[2]
    s = s + s_part(1)
    sum_start(1, 0, fold(quarters(s)))
    a = factor_start(unfold(sum_finish(0, 1)) * (1.0 / ntot))
    a = factor_steps(a, 0, half)
    sum_start(1, 1, sum_finish(1, 0))
    a = factor_steps(a, half, n)
    li = factor_end(a)
    li_hi, li_lo = split(li)
    ll = jnp.concatenate([jnp.concatenate([li_hi, li_hi], axis=1), jnp.concatenate([li_lo, li_lo], axis=1)], axis=0)
    for j in range(L // CH):
        at = slice(j * CH, (j + 1) * CH)
        for k, src in enumerate((zz, zzp)):
            v = mm(ll, src[:, at], NN)
            ostage[k, :, at] = v[:n] + v[n:]
    orows = pl.multiple_of((1 - h) * half, half)
    ocopy = []
    for k, out in enumerate((nc, nd)):
        ocopy.append(remote(ostage.at[k, pl.ds(orows, half)], out.at[:, pl.ds(mine, L)], outs.at[k], outr.at[k], sib))
        ocopy.append(pltpu.make_async_copy(ostage.at[k, pl.ds(hrows, half)], out.at[:, pl.ds(mine, L)], loc_sem.at[2 + k]))
    for c in ocopy:
        c.start()
    s = unfold(sum_finish(1, 1)) * (1.0 / ntot)
    sym = s + jnp.transpose(s)
    proj[...] = mm_high(mm_high(li, sym, NN), li, NT)
    for c in ocopy:
        c.wait()
    for c in xcopy + shared[1:2] + [zcopy] + scopy + bcopy + tcopy:
        c.wait_send()
    pl.when(h == 1)(shared[0].wait_send)
    pl.when(h == 0)(shared[2].wait_send)


def place(*refs):
    for k in range(3):
        refs[3 + k][...] = refs[k][...]


def on_device(dims, ntot, blocks, columns, current, directions, ritz_values, rotation):
    rows_here, slots = columns.shape
    half, length = current.shape
    states = rotation.shape[1]
    total_rows = ntot // W
    rows = lax.axis_index("row") * rows_here + jnp.arange(rows_here, dtype=jnp.int32)
    offsets = jnp.mod(columns - rows[:, None], total_rows)
    hit = offsets[:, None, :] == jnp.arange(WB + 1, dtype=jnp.int32)[None, :, None]
    inv = slots + jnp.sum(jnp.where(hit, jnp.arange(slots, dtype=jnp.int32) - slots, 0), axis=2)

    any_ = pl.BlockSpec(memory_space=pl.ANY)
    vmem = pl.BlockSpec(memory_space=pltpu.VMEM)
    smem = pl.BlockSpec(memory_space=pltpu.SMEM)
    ga = 2 * dims[-1]
    gb = total_rows // rows_here // dims[-1]
    dma = pltpu.SemaphoreType.DMA
    scratch = [pltpu.VMEM((slots + 1, W, W), F32) for _ in range(RB)] + [
        pltpu.VMEM((L, SLABS * L), BF16),
        pltpu.VMEM((L, SLABS * L), BF16),
        pltpu.VMEM((SLABS + 1, states, L), F32),
        pltpu.VMEM((SLABS, 2 * states, L), BF16),
        pltpu.VMEM((2, states, L), F32),
        pltpu.VMEM((2 * states, L), BF16),
        pltpu.VMEM((2 * states, L), BF16),
        pltpu.VMEM((SLABS, states, L), F32),
        pltpu.VMEM((SLABS, states, L), F32),
        pltpu.VMEM((SLABS, states, L), F32),
        pltpu.VMEM((3, states, L), F32),
        pltpu.VMEM((states, L), F32),
        pltpu.VMEM((states, L), F32),
        pltpu.VMEM((states, W), F32),
        pltpu.VMEM((states, 3 * states), F32),
        pltpu.VMEM((1, half), F32),
        pltpu.VMEM((2, states, L), F32),
        pltpu.VMEM((2, ga, half, 2 * states), F32),
        pltpu.VMEM((2, gb, half, 2 * states), F32),
        dma((RB,)), dma((6,)), dma((3,)), dma((3,)),
        dma((2,)), dma((2,)), dma((3,)), dma((3,)), dma(()), dma(()), dma((3,)), dma((3,)),
        dma((SLABS,)), dma((SLABS,)),
        dma((2, ga)), dma((2, ga)), dma((2, gb)), dma((2, gb)), dma((2,)), dma((2,)),
    ]
    outs = pl.pallas_call(
        functools.partial(kernel, dims, ntot),
        out_shape=(
            jax.ShapeDtypeStruct((half, length), F32),
            jax.ShapeDtypeStruct((half, length), F32),
            jax.ShapeDtypeStruct((states, states), F32),
        ),
        in_specs=[smem, any_, any_, any_, any_, any_],
        out_specs=(any_, any_, vmem),
        scratch_shapes=scratch,
        compiler_params=pltpu.CompilerParams(
            collective_id=0, has_side_effects=True, vmem_limit_bytes=58 * 2**20
        ),
        name="lobpcg",
    )(inv, blocks, current, directions, ritz_values.reshape(1, half), rotation.T)
    return pl.pallas_call(
        place,
        out_shape=tuple(jax.ShapeDtypeStruct(o.shape, o.dtype) for o in outs),
        in_specs=[vmem] * 3,
        out_specs=(vmem,) * 3,
        name="place",
    )(*outs)


def solution(mesh):
    rows_n = mesh.shape["row"]
    side = round(rows_n ** (1 / 3))
    dims = (side, side, rows_n // (side * side))
    in_specs = (
        P("row", None, None, None),
        P("row", None),
        P("col", "row"),
        P("col", "row"),
        P("col"),
        P(),
    )
    out_specs = (P("col", "row"), P("col", "row"), P())
    ntot = rows_n * 2 * L
    return jax.shard_map(
        functools.partial(on_device, dims, ntot), mesh=mesh, in_specs=in_specs, out_specs=out_specs, check_vma=False
    )
```

```python
import functools

import jax
import jax.numpy as jnp
from jax import lax
from jax.experimental import pallas as pl
from jax.experimental.pallas import tpu as pltpu
from jax.sharding import PartitionSpec as P

WB = 32
F32 = jnp.float32
BF16 = jnp.bfloat16
MESH = pl.DeviceIdType.MESH
NN = (((1,), (0,)), ((), ()))
NT = (((1,), (1,)), ((), ()))
TN = (((0,), (0,)), ((), ()))
HIGH = lax.Precision.HIGHEST

RB = 8
W = 128
L = RB * W
SLABS = WB // RB + 1
CH = 256


def mm(a, b, dims):
    return lax.dot_general(a, b, dims, preferred_element_type=F32)


def mm_high(a, b, dims):
    return lax.dot_general(a, b, dims, precision=HIGH, preferred_element_type=F32)


def split(v):
    hi = v.astype(BF16)
    return hi, (v - hi.astype(F32)).astype(BF16)


def factor_start(g):
    n = g.shape[0]
    rows = lax.broadcasted_iota(jnp.int32, (n, 2 * n), 0)
    lanes = lax.broadcasted_iota(jnp.int32, (n, 2 * n), 1)
    a = jnp.concatenate([g, jnp.zeros((n, n), F32)], axis=1) + jnp.where(rows + n == lanes, 1.0, 0.0).astype(F32)
    return [a[8 * i:8 * i + 8] for i in range(n // 8)]


def factor_steps(a, first, last):
    a = list(a)
    sub = lax.broadcasted_iota(jnp.int32, (8, 1), 0)
    for k in range(first, last):
        b, s = divmod(k, 8)
        row = a[b][s:s + 1, :]
        scaled = row * (1.0 / row[:, k:k + 1])
        for i in range(b, len(a)):
            col = a[i][:, k:k + 1]
            if i == b:
                col = jnp.where(sub > s, col, 0.0)
            a[i] = a[i] - col * scaled
    return a


def factor_end(a):
    a = jnp.concatenate(a, axis=0)
    n = a.shape[0]
    rows = lax.broadcasted_iota(jnp.int32, (n, 2 * n), 0)
    lanes = lax.broadcasted_iota(jnp.int32, (n, 2 * n), 1)
    diag = jnp.sum(jnp.where(rows == lanes, a, 0.0), axis=1, keepdims=True)
    return a[:, n:] * (1.0 / jnp.sqrt(diag))


def kernel(dims, ntot, columns, blocks, current, directions, ritz, rot, nc, nd, proj, *scratch):
    stages = scratch[:RB]
    (mh, ml, xw, xx, zw, zz, zzp, part, inbuf, tb, tin, hx, pv, lam, rotv, ritzv, colv, invv, inv_ref, xo, ostage, bufa, bufb,
     blk_sem, loc_sem, exs, exr, xs, xr, cs, cr, zs, zr, ts, tr, ss, sr, bs, br, asa, ara, asb, arb, outs, outr) = scratch[RB:]
    half, full = current.shape
    slots = blocks.shape[1]
    rows_n = 1
    for m in dims:
        rows_n *= m
    r = lax.axis_index("row")
    h = lax.axis_index("col")
    sib = (r, 1 - h)

    ny = dims[-1]
    nb = rows_n // ny
    y = lax.rem(r, ny)
    groups = [
        (2 * ny, 2 * y + h, lambda k: (r - y + k // 2, lax.rem(k, 2)), (bufa, asa, ara)),
        (nb, r // ny, lambda k: (k * ny + y, h), (bufb, asb, arb)),
    ]

    def row_at(k):
        return (lax.rem(r + k + rows_n, rows_n), h)

    barrier = pltpu.get_barrier_semaphore()
    partners = [row_at(k) for k in (-1, 1)]
    for m, c, member, _ in groups:
        for k in range(1, m):
            partners.append(member(lax.rem(c + k, m)))
    for d in partners:
        pl.semaphore_signal(barrier, inc=1, device_id=d, device_id_type=MESH)

    for i in range(RB):
        pltpu.make_async_copy(
            blocks.at[h * RB + i], stages[i].at[pl.ds(0, slots)], blk_sem.at[i]
        ).start()
    mine = pl.multiple_of(h * L, L)
    other = pl.multiple_of((1 - h) * L, L)
    hrows = pl.multiple_of(h * half, half)
    loc_x = pltpu.make_async_copy(current.at[:, pl.ds(mine, L)], xw.at[h, pl.ds(hrows, half)], loc_sem.at[0])
    loc_x.start()
    loc_p = pltpu.make_async_copy(directions.at[:, pl.ds(mine, L)], pv.at[pl.ds(hrows, half)], loc_sem.at[1])
    loc_p.start()
    loc_xo = pltpu.make_async_copy(current.at[:, pl.ds(other, L)], xo, loc_sem.at[8])
    loc_xo.start()
    loc_rot = pltpu.make_async_copy(rot, rotv, loc_sem.at[4])
    loc_rot.start()
    loc_ritz = pltpu.make_async_copy(ritz, ritzv, loc_sem.at[5])
    loc_ritz.start()
    loc_col = pltpu.make_async_copy(columns, colv, loc_sem.at[6])
    loc_col.start()

    for i in range(RB):
        stages[i][slots] = jnp.zeros((W, W), F32)
    zero = jnp.zeros((W, W), BF16)
    for j in range(0, RB, 2):
        for m_ref in (mh, ml):
            m_ref[(j + 1) * W:(j + 2) * W, j * W:(j + 1) * W] = zero
            m_ref[j * W:(j + 1) * W, (WB + j + 1) * W:(WB + j + 2) * W] = zero
    loc_col.wait()
    at = lax.broadcasted_iota(jnp.int32, (RB, slots), 0) + (2 * r + h) * RB
    ahead = colv[pl.ds(pl.multiple_of(h * RB, RB), RB), :] - at
    ahead = jnp.where(ahead < 0, ahead + rows_n * 2 * RB, ahead)
    lanes = lax.broadcasted_iota(jnp.int32, (RB, W), 1)
    found = jnp.full((RB, W), slots, jnp.int32)
    for k in range(slots):
        found = jnp.where(ahead[:, k:k + 1] == lanes, k, found)
    invv[...] = found
    to_smem = pltpu.make_async_copy(invv, inv_ref, loc_sem.at[7])
    to_smem.start()
    to_smem.wait()
    loc_xo.wait()
    pl.semaphore_wait(barrier, len(partners))

    def remote(src, dst, ssem, rsem, dev):
        return pltpu.make_async_remote_copy(
            src_ref=src, dst_ref=dst, send_sem=ssem, recv_sem=rsem, device_id=dev, device_id_type=MESH)

    ex = [
        remote(xo, xw.at[1 - h, pl.ds(hrows, half)], exs.at[0], exr.at[0], sib),
        remote(directions.at[:, pl.ds(other, L)], pv.at[pl.ds(hrows, half)], exs.at[1], exr.at[1], sib),
        remote(lam.at[pl.ds(hrows, half)], lam.at[pl.ds(hrows, half)], exs.at[2], exr.at[2], sib),
    ]
    for c in ex[:2]:
        c.start()
    piece = [pl.ds(c * half, half) for c in range(2)]

    def pieces(src, i, dst, j, ssem, rsem, first, dev):
        return [remote(src.at[i, p], dst.at[j, p], ssem.at[first + c], rsem.at[first + c], dev) for c, p in enumerate(piece)]

    xown = pieces(xw, h, xw, h + 2, xs, xr, 0, row_at(-1))
    xpass = pieces(xw, h + 2, xw, h + 4, xs, xr, 2, row_at(-1))
    shared = [remote(xw.at[w], xw.at[w], cs.at[k], cr.at[k], sib) for k, w in enumerate((1, 2 + h, 4))]
    got = remote(xw.at[3 - h], xw.at[3 - h], cs.at[1], cr.at[1], sib)
    zcopy = remote(zw.at[0], zw.at[1], zs, zr, row_at(-1))
    tcopy = [remote(tb.at[t], tin.at[k], ts.at[k], tr.at[k], dev) for k, (t, dev) in enumerate(((1, sib), (3, sib), (4, row_at(1))))]
    scopy = [remote(part.at[t], inbuf.at[t], ss.at[t // 2], sr.at[t // 2], sib) for t in (1, 3)]
    bown = pieces(part, 4, inbuf, 4, bs, br, 0, row_at(1))
    bpass = pieces(part, 2, inbuf, 2, bs, br, 2, row_at(1))

    def to_parts(t):
        hi, lo = split(xw[h + t])
        xx[t, :2 * half] = hi
        xx[t, 2 * half:] = lo

    def expand(i):
        pltpu.make_async_copy(
            blocks.at[h * RB + i], stages[i].at[pl.ds(0, slots)], blk_sem.at[i]
        ).wait()
        hi, lo = split(stages[i][0] * 0.5)
        mh[i * W:(i + 1) * W, i * W:(i + 1) * W] = hi
        ml[i * W:(i + 1) * W, i * W:(i + 1) * W] = lo

        def one(d, carry):
            hi, lo = split(stages[i][inv_ref[i, d]])
            at = pl.multiple_of((i + d) * W, W)
            mh[i * W:(i + 1) * W, pl.ds(at, W)] = hi
            ml[i * W:(i + 1) * W, pl.ds(at, W)] = lo
            return carry

        lax.fori_loop(1, WB + 1, one, 0, unroll=4)

    def times_m(src, t, write):
        def chunk(j, lo, hi):
            at = pl.multiple_of(t * L + j * CH, CH)
            a = mm(src[:, lo:hi], mh[lo:hi, pl.ds(at, CH)], NN)
            b = mm(src[:2 * half, lo:hi], ml[lo:hi, pl.ds(at, CH)], NN)
            write(pl.ds(pl.multiple_of(j * CH, CH), CH), a[:2 * half] + a[2 * half:] + b)

        if t == 0 or t == SLABS - 1:
            for j in range(L // CH):
                chunk(j, *((0, (j + 1) * CH) if t == 0 else (j * CH, L)))
        else:
            def body(j, carry):
                chunk(j, 0, L)
                return carry
            lax.fori_loop(0, L // CH, body, 0, unroll=True)

    def times_mt(t):
        def chunk(j, lo, hi):
            at = pl.ds(pl.multiple_of(j * CH, CH), CH)
            a = mm(xx[t, :, lo:hi], mh[at, t * L + lo:t * L + hi], NT)
            b = mm(xx[t, :2 * half, lo:hi], ml[at, t * L + lo:t * L + hi], NT)
            hx[:, at] += a[:2 * half] + a[2 * half:] + b

        if t == 0 or t == SLABS - 1:
            for j in range(L // CH):
                chunk(j, *((j * CH, L) if t == 0 else (0, (j + 1) * CH)))
        else:
            def body(j, carry):
                chunk(j, 0, L)
                return carry
            lax.fori_loop(0, L // CH, body, 0, unroll=True)

    def back(t):
        def put(at, v):
            part[t, :, at] = v
        times_m(xx.at[0], t, put)

    loc_x.wait()
    for i in range(RB // 2):
        expand(i)
    ex[0].wait()
    for c in xown:
        c.start()
    pl.when(h == 1)(shared[0].start)
    for i in range(RB // 2, RB):
        expand(i)
    to_parts(0)
    er = lax.broadcasted_iota(jnp.int32, (half, half), 0) == lax.broadcasted_iota(jnp.int32, (half, half), 1)
    loc_ritz.wait()
    lam_own = jnp.sum(jnp.where(er, jnp.broadcast_to(ritzv[...], (half, half)), 0.0), axis=1, keepdims=True)
    lam[pl.ds(hrows, half), :] = jnp.broadcast_to(lam_own, (half, W))
    ex[2].start()
    back(3)
    scopy[1].start()
    back(4)

    @pl.when(h == 0)
    def _():
        scopy[1].wait_recv()
        part[4] += inbuf[3]
    for c in bown:
        c.start()
    back(1)
    scopy[0].start()
    back(2)
    xown[0].wait_recv()
    xpass[0].start()

    @pl.when(h == 0)
    def _():
        scopy[0].wait_recv()
        part[2] += inbuf[1]

    @pl.when(h == 1)
    def _():
        scopy[1].wait_recv()
        part[2] += inbuf[3]

    def pass_products(c):
        bown[c].wait_recv()
        part[2, piece[c]] += inbuf[4, piece[c]]
        bpass[c].start()

    def put_hx(at, v):
        hx[:, at] = v
    times_m(xx.at[0], 0, put_hx)
    times_mt(0)
    xown[1].wait_recv()
    xpass[1].start()
    shared[1].start()
    pl.when(h == 0)(shared[0].wait_recv)
    pl.when(h == 1)(got.wait_recv)
    to_parts(1)
    times_mt(1)
    pass_products(0)
    to_parts(2)
    times_mt(2)
    pass_products(1)
    for c in xpass:
        c.wait_recv()
    pl.when(h == 0)(shared[2].start)
    to_parts(4)
    times_mt(4)
    pl.when(h == 0)(got.wait_recv)
    pl.when(h == 1)(shared[2].wait_recv)
    to_parts(3)
    times_mt(3)
    loc_p.wait()
    ex[1].wait()
    ex[2].wait()
    @pl.when(h == 1)
    def _():
        scopy[0].wait_recv()
        hx[...] += inbuf[1]
    for c in bpass:
        c.wait_recv()

    loc_rot.wait()
    n = 2 * half
    ct_hi, ct_lo = split(jnp.concatenate(
        [rotv[...], jnp.where(lax.broadcasted_iota(jnp.int32, (n, 3 * n), 1) < n, 0.0, rotv[...])], axis=0))
    ct = jnp.concatenate([ct_hi, ct_lo], axis=0)
    for j in range(L // CH):
        at = slice(j * CH, (j + 1) * CH)
        x = xw[h, :, at]
        res = hx[:, at] + inbuf[2, :, at] - jnp.concatenate([lam[...]] * (CH // W), axis=1) * x
        r_hi, r_lo = split(res)
        p_hi, p_lo = split(pv[:, at])
        b_hi = jnp.concatenate([xx[0, :n, at], r_hi, p_hi], axis=0)
        b_lo = jnp.concatenate([xx[0, n:, at], r_lo, p_lo], axis=0)
        both = mm(ct, b_hi, NN)
        both = both[:2 * n] + both[2 * n:] + mm(ct_hi, b_lo, NN)
        zw[0, :, at] = both[:n]
        hi, lo = split(both[:n])
        zz[:n, at] = hi
        zz[n:, at] = lo
        hi, lo = split(both[n:])
        zzp[:n, at] = hi
        zzp[n:, at] = lo

    def sum_copies(which, g):
        m, c, member, (buf, ssem, rsem) = groups[g]
        return [
            remote(buf.at[which, c], buf.at[which, c], ssem.at[which, k - 1], rsem.at[which, k - 1],
                   member(lax.rem(c + k, m)))
            for k in range(1, m)
        ]

    def sum_start(which, g, value):
        m, c, member, (buf, ssem, rsem) = groups[g]
        buf[which, c] = value
        for copy in sum_copies(which, g):
            copy.start()

    def sum_finish(which, g):
        m, c, member, (buf, ssem, rsem) = groups[g]
        for copy in sum_copies(which, g):
            copy.wait()
        total = buf[which, 0]
        for k in range(1, m):
            total = total + buf[which, k]
        return total

    def z_times_m(t):
        def put(at, v):
            tb[t, :, at] = v
        times_m(zz, t, put)

    def quarters(v):
        return v[:n, :n] + v[:n, n:] + v[n:, :n] + v[n:, n:]

    def s_part(k):
        if k:
            hi, lo = split(zw[k])
            other_z = jnp.concatenate([hi, lo], axis=0)
        else:
            other_z = zz[...]
        hi, lo = split(tb[2 * k])
        return mm(jnp.concatenate([hi, lo], axis=0), other_z, NT)

    def fold(v):
        return jnp.concatenate([v[:half], v[half:]], axis=1)

    def unfold(v):
        return jnp.concatenate([v[:, :n], v[:, n:]], axis=0)

    z_times_m(3)
    tcopy[1].start()
    sum_start(0, 0, fold(quarters(mm(zz[...], zz[...], NT))))
    zcopy.start()
    z_times_m(4)
    tcopy[1].wait_recv()

    @pl.when(h == 0)
    def _():
        tb[4] += tin[1]
    tcopy[2].start()
    z_times_m(1)
    tcopy[0].start()
    sum_start(0, 1, sum_finish(0, 0))
    z_times_m(0)
    z_times_m(2)
    tcopy[0].wait_recv()
    tb[2 * (1 - h)] += tin[0]

    @pl.when(h == 1)
    def _():
        tb[2] += tin[1]
    s = s_part(0)
    zcopy.wait_recv()
    tcopy[2].wait_recv()
    tb[2] += tin[2]
    s = s + s_part(1)
    sum_start(1, 0, fold(quarters(s)))
    a = factor_start(unfold(sum_finish(0, 1)) * (1.0 / ntot))
    a = factor_steps(a, 0, half)
    sum_start(1, 1, sum_finish(1, 0))
    a = factor_steps(a, half, n)
    li = factor_end(a)
    li_hi, li_lo = split(li)
    ll = jnp.concatenate([jnp.concatenate([li_hi, li_hi], axis=1), jnp.concatenate([li_lo, li_lo], axis=1)], axis=0)
    for j in range(L // CH):
        at = slice(j * CH, (j + 1) * CH)
        for k, src in enumerate((zz, zzp)):
            v = mm(ll, src[:, at], NN)
            ostage[k, :, at] = v[:n] + v[n:]
    orows = pl.multiple_of((1 - h) * half, half)
    ocopy = []
    for k, out in enumerate((nc, nd)):
        ocopy.append(remote(ostage.at[k, pl.ds(orows, half)], out.at[:, pl.ds(mine, L)], outs.at[k], outr.at[k], sib))
        ocopy.append(pltpu.make_async_copy(ostage.at[k, pl.ds(hrows, half)], out.at[:, pl.ds(mine, L)], loc_sem.at[2 + k]))
    for c in ocopy:
        c.start()
    s = unfold(sum_finish(1, 1)) * (1.0 / ntot)
    sym = s + jnp.transpose(s)
    proj[...] = mm_high(mm_high(li, sym, NN), li, NT)
    for c in ocopy:
        c.wait()
    for c in xown + xpass + shared[1:2] + [zcopy] + scopy + bown + bpass + tcopy:
        c.wait_send()
    pl.when(h == 1)(shared[0].wait_send)
    pl.when(h == 0)(shared[2].wait_send)


def place(*refs):
    for k in range(3):
        refs[3 + k][...] = refs[k][...]


def on_device(dims, ntot, blocks, columns, current, directions, ritz_values, rotation):
    rows_here, slots = columns.shape
    half, length = current.shape
    states = rotation.shape[1]
    total_rows = ntot // W
    any_ = pl.BlockSpec(memory_space=pl.ANY)
    vmem = pl.BlockSpec(memory_space=pltpu.VMEM)
    ga = 2 * dims[-1]
    gb = total_rows // rows_here // dims[-1]
    dma = pltpu.SemaphoreType.DMA
    scratch = [pltpu.VMEM((slots + 1, W, W), F32) for _ in range(RB)] + [
        pltpu.VMEM((L, SLABS * L), BF16),
        pltpu.VMEM((L, SLABS * L), BF16),
        pltpu.VMEM((SLABS + 1, states, L), F32),
        pltpu.VMEM((SLABS, 2 * states, L), BF16),
        pltpu.VMEM((2, states, L), F32),
        pltpu.VMEM((2 * states, L), BF16),
        pltpu.VMEM((2 * states, L), BF16),
        pltpu.VMEM((SLABS, states, L), F32),
        pltpu.VMEM((SLABS, states, L), F32),
        pltpu.VMEM((SLABS, states, L), F32),
        pltpu.VMEM((3, states, L), F32),
        pltpu.VMEM((states, L), F32),
        pltpu.VMEM((states, L), F32),
        pltpu.VMEM((states, W), F32),
        pltpu.VMEM((states, 3 * states), F32),
        pltpu.VMEM((1, half), F32),
        pltpu.VMEM((rows_here, slots), jnp.int32),
        pltpu.VMEM((RB, W), jnp.int32),
        pltpu.SMEM((RB, W), jnp.int32),
        pltpu.VMEM((half, L), F32),
        pltpu.VMEM((2, states, L), F32),
        pltpu.VMEM((2, ga, half, 2 * states), F32),
        pltpu.VMEM((2, gb, half, 2 * states), F32),
        dma((RB,)), dma((9,)), dma((3,)), dma((3,)),
        dma((4,)), dma((4,)), dma((3,)), dma((3,)), dma(()), dma(()), dma((3,)), dma((3,)),
        dma((2,)), dma((2,)), dma((4,)), dma((4,)),
        dma((2, ga)), dma((2, ga)), dma((2, gb)), dma((2, gb)), dma((2,)), dma((2,)),
    ]
    outs = pl.pallas_call(
        functools.partial(kernel, dims, ntot),
        out_shape=(
            jax.ShapeDtypeStruct((half, length), F32),
            jax.ShapeDtypeStruct((half, length), F32),
            jax.ShapeDtypeStruct((states, states), F32),
        ),
        in_specs=[any_, any_, any_, any_, any_, any_],
        out_specs=(any_, any_, vmem),
        scratch_shapes=scratch,
        compiler_params=pltpu.CompilerParams(
            collective_id=0, has_side_effects=True, vmem_limit_bytes=58 * 2**20
        ),
        name="lobpcg",
    )(columns, blocks, current, directions, ritz_values.reshape(1, half), rotation.T)
    return pl.pallas_call(
        place,
        out_shape=tuple(jax.ShapeDtypeStruct(o.shape, o.dtype) for o in outs),
        in_specs=[vmem] * 3,
        out_specs=(vmem,) * 3,
        name="place",
    )(*outs)


def solution(mesh):
    rows_n = mesh.shape["row"]
    side = round(rows_n ** (1 / 3))
    dims = (side, side, rows_n // (side * side))
    in_specs = (
        P("row", None, None, None),
        P("row", None),
        P("col", "row"),
        P("col", "row"),
        P("col"),
        P(),
    )
    out_specs = (P("col", "row"), P("col", "row"), P())
    ntot = rows_n * 2 * L
    return jax.shard_map(
        functools.partial(on_device, dims, ntot), mesh=mesh, in_specs=in_specs, out_specs=out_specs, check_vma=False
    )
```

```python
import functools

import jax
import jax.numpy as jnp
from jax import lax
from jax.experimental import pallas as pl
from jax.experimental.pallas import tpu as pltpu
from jax.sharding import PartitionSpec as P

WB = 32
F32 = jnp.float32
BF16 = jnp.bfloat16
MESH = pl.DeviceIdType.MESH
NN = (((1,), (0,)), ((), ()))
NT = (((1,), (1,)), ((), ()))
TN = (((0,), (0,)), ((), ()))

RB = 8
W = 128
L = RB * W
SLABS = WB // RB + 1
CH = 256
PIECES = 4


def mm(a, b, dims):
    return lax.dot_general(a, b, dims, preferred_element_type=F32)


def split(v):
    hi = v.astype(BF16)
    return hi, (v - hi.astype(F32)).astype(BF16)


def factor_start(g):
    n = g.shape[0]
    rows = lax.broadcasted_iota(jnp.int32, (n, 2 * n), 0)
    lanes = lax.broadcasted_iota(jnp.int32, (n, 2 * n), 1)
    a = jnp.concatenate([g, jnp.zeros((n, n), F32)], axis=1) + jnp.where(rows + n == lanes, 1.0, 0.0).astype(F32)
    return [a[8 * i:8 * i + 8] for i in range(n // 8)]


def factor_steps(a, first, last):
    a = list(a)
    sub = lax.broadcasted_iota(jnp.int32, (8, 1), 0)
    for k in range(first, last):
        b, s = divmod(k, 8)
        row = a[b][s:s + 1, :]
        scaled = row * (1.0 / row[:, k:k + 1])
        for i in range(b, len(a)):
            col = a[i][:, k:k + 1]
            if i == b:
                col = jnp.where(sub > s, col, 0.0)
            a[i] = a[i] - col * scaled
    return a


def factor_end(a):
    a = jnp.concatenate(a, axis=0)
    n = a.shape[0]
    rows = lax.broadcasted_iota(jnp.int32, (n, 2 * n), 0)
    lanes = lax.broadcasted_iota(jnp.int32, (n, 2 * n), 1)
    diag = jnp.sum(jnp.where(rows == lanes, a, 0.0), axis=1, keepdims=True)
    return a[:, n:] * (1.0 / jnp.sqrt(diag))


def kernel(dims, ntot, columns, blocks, current, directions, ritz, rot, nc, nd, proj, *scratch):
    stages = scratch[:RB]
    (mh, ml, xw, xx, zw, zz, zzp, part, inbuf, tb, tin, hx, pv, lam, rotv, ritzv, colv, invv, inv_ref, ostage, bufa, bufb,
     blk_sem, loc_sem, exs, exr, xs, xr, cs, cr, zs, zr, ts, tr, ss, sr, bs, br, asa, ara, asb, arb, outs, outr) = scratch[RB:]
    half, full = current.shape
    slots = blocks.shape[1]
    rows_n = 1
    for m in dims:
        rows_n *= m
    r = lax.axis_index("row")
    h = lax.axis_index("col")
    sib = (r, 1 - h)

    ny = dims[-1]
    nb = rows_n // ny
    y = lax.rem(r, ny)
    groups = [
        (2 * ny, 2 * y + h, lambda k: (r - y + k // 2, lax.rem(k, 2)), (bufa, asa, ara)),
        (nb, r // ny, lambda k: (k * ny + y, h), (bufb, asb, arb)),
    ]

    def row_at(k):
        return (lax.rem(r + k + rows_n, rows_n), h)

    barrier = pltpu.get_barrier_semaphore()
    partners = [row_at(k) for k in (-1, 1)]
    for m, c, member, _ in groups:
        for k in range(1, m):
            partners.append(member(lax.rem(c + k, m)))
    for d in partners:
        pl.semaphore_signal(barrier, inc=1, device_id=d, device_id_type=MESH)

    for i in range(RB):
        pltpu.make_async_copy(
            blocks.at[h * RB + i], stages[i].at[pl.ds(0, slots)], blk_sem.at[i]
        ).start()
    mine = pl.multiple_of(h * L, L)
    other = pl.multiple_of((1 - h) * L, L)
    hrows = pl.multiple_of(h * half, half)
    loc_x = [
        pltpu.make_async_copy(current.at[:, pl.ds(w * L, L)], xw.at[w, pl.ds(hrows, half)], loc_sem.at[8 * w])
        for w in range(2)
    ]
    for c in loc_x:
        c.start()
    loc_p = pltpu.make_async_copy(directions.at[:, pl.ds(mine, L)], pv.at[pl.ds(hrows, half)], loc_sem.at[1])
    loc_p.start()
    loc_rot = pltpu.make_async_copy(rot, rotv, loc_sem.at[4])
    loc_rot.start()
    loc_ritz = pltpu.make_async_copy(ritz, ritzv, loc_sem.at[5])
    loc_ritz.start()
    loc_col = pltpu.make_async_copy(columns, colv, loc_sem.at[6])
    loc_col.start()

    for i in range(RB):
        stages[i][slots] = jnp.zeros((W, W), F32)
    zero = jnp.zeros((W, W), BF16)
    for j in range(0, RB, 2):
        for m_ref in (mh, ml):
            m_ref[(j + 1) * W:(j + 2) * W, j * W:(j + 1) * W] = zero
            m_ref[j * W:(j + 1) * W, (WB + j + 1) * W:(WB + j + 2) * W] = zero
    loc_col.wait()
    at = lax.broadcasted_iota(jnp.int32, (RB, slots), 0) + (2 * r + h) * RB
    ahead = colv[pl.ds(pl.multiple_of(h * RB, RB), RB), :] - at
    ahead = jnp.where(ahead < 0, ahead + rows_n * 2 * RB, ahead)
    lanes = lax.broadcasted_iota(jnp.int32, (RB, W), 1)
    found = jnp.full((RB, W), slots, jnp.int32)
    for k in range(slots):
        found = jnp.where(ahead[:, k:k + 1] == lanes, k, found)
    invv[...] = found
    to_smem = pltpu.make_async_copy(invv, inv_ref, loc_sem.at[7])
    to_smem.start()
    to_smem.wait()
    for c in loc_x:
        c.wait()
    pl.semaphore_wait(barrier, len(partners))

    def remote(src, dst, ssem, rsem, dev):
        return pltpu.make_async_remote_copy(
            src_ref=src, dst_ref=dst, send_sem=ssem, recv_sem=rsem, device_id=dev, device_id_type=MESH)

    ex = [
        remote(xw.at[1 - h, pl.ds(hrows, half)], xw.at[1 - h, pl.ds(hrows, half)], exs.at[0], exr.at[0], sib),
        remote(directions.at[:, pl.ds(other, L)], pv.at[pl.ds(hrows, half)], exs.at[1], exr.at[1], sib),
        remote(lam.at[pl.ds(hrows, half)], lam.at[pl.ds(hrows, half)], exs.at[2], exr.at[2], sib),
    ]
    ex[0].start()
    piece = [pl.ds(c * (2 * half // PIECES), 2 * half // PIECES) for c in range(PIECES)]

    def pieces(src, i, dst, j, ssem, rsem, first, dev):
        return [remote(src.at[i, p], dst.at[j, p], ssem.at[first + c], rsem.at[first + c], dev) for c, p in enumerate(piece)]

    def x_piece(c, w):
        return xw.at[w, pl.ds(pl.multiple_of(hrows + c % 2 * (half // 2), half // 2), half // 2)]

    xown = [remote(x_piece(c, c // 2), x_piece(c, c // 2 + 2), xs.at[c], xr.at[c], row_at(-1)) for c in range(PIECES)]
    xpass = [
        remote(x_piece(c, c // 2 + 2), x_piece(c, c // 2 + 4), xs.at[PIECES + c], xr.at[PIECES + c], row_at(-1))
        for c in range(PIECES)
    ]
    shared = [
        remote(xw.at[w, pl.ds(hrows, half)], xw.at[w, pl.ds(hrows, half)], cs.at[w - 1], cr.at[w - 1], sib)
        for w in range(1, SLABS + 1)
    ]
    for c in xown:
        c.start()
    pl.when(h == 1)(shared[0].start)
    ex[1].start()
    zcopy = remote(zw.at[0], zw.at[1], zs, zr, row_at(-1))
    tcopy = [remote(tb.at[t], tin.at[k], ts.at[k], tr.at[k], dev) for k, (t, dev) in enumerate(((1, sib), (3, sib), (4, row_at(1))))]
    scopy = [remote(part.at[t], inbuf.at[t], ss.at[t // 2], sr.at[t // 2], sib) for t in (1, 3)]
    bown = pieces(part, 4, inbuf, 4, bs, br, 0, row_at(1))
    bpass = pieces(part, 2, inbuf, 2, bs, br, PIECES, row_at(1))

    def to_parts(t):
        hi, lo = split(xw[h + t])
        xx[t, :2 * half] = hi
        xx[t, 2 * half:] = lo

    def expand(i):
        pltpu.make_async_copy(
            blocks.at[h * RB + i], stages[i].at[pl.ds(0, slots)], blk_sem.at[i]
        ).wait()
        hi, lo = split(stages[i][0] * 0.5)
        mh[i * W:(i + 1) * W, i * W:(i + 1) * W] = hi
        ml[i * W:(i + 1) * W, i * W:(i + 1) * W] = lo

        def one(d, carry):
            hi, lo = split(stages[i][inv_ref[i, d]])
            at = pl.multiple_of((i + d) * W, W)
            mh[i * W:(i + 1) * W, pl.ds(at, W)] = hi
            ml[i * W:(i + 1) * W, pl.ds(at, W)] = lo
            return carry

        lax.fori_loop(1, WB + 1, one, 0, unroll=4)

    def times_m(src, t, write):
        def chunk(j, lo, hi):
            at = pl.multiple_of(t * L + j * CH, CH)
            a = mm(src[:, lo:hi], mh[lo:hi, pl.ds(at, CH)], NN)
            b = mm(src[:2 * half, lo:hi], ml[lo:hi, pl.ds(at, CH)], NN)
            write(pl.ds(pl.multiple_of(j * CH, CH), CH), a[:2 * half] + a[2 * half:] + b)

        if t == 0 or t == SLABS - 1:
            for j in range(L // CH):
                chunk(j, *((0, (j + 1) * CH) if t == 0 else (j * CH, L)))
        else:
            def body(j, carry):
                chunk(j, 0, L)
                return carry
            lax.fori_loop(0, L // CH, body, 0, unroll=True)

    def times_mt(t):
        def chunk(j, lo, hi):
            at = pl.ds(pl.multiple_of(j * CH, CH), CH)
            a = mm(xx[t, :, lo:hi], mh[at, t * L + lo:t * L + hi], NT)
            b = mm(xx[t, :2 * half, lo:hi], ml[at, t * L + lo:t * L + hi], NT)
            hx[:, at] += a[:2 * half] + a[2 * half:] + b

        if t == 0 or t == SLABS - 1:
            for j in range(L // CH):
                chunk(j, *((j * CH, L) if t == 0 else (0, (j + 1) * CH)))
        else:
            def body(j, carry):
                chunk(j, 0, L)
                return carry
            lax.fori_loop(0, L // CH, body, 0, unroll=True)

    def back(t):
        def put(at, v):
            part[t, :, at] = v
        times_m(xx.at[0], t, put)

    for i in range(RB):
        expand(i)
    ex[0].wait()
    to_parts(0)
    er = lax.broadcasted_iota(jnp.int32, (half, half), 0) == lax.broadcasted_iota(jnp.int32, (half, half), 1)
    loc_ritz.wait()
    lam_own = jnp.sum(jnp.where(er, jnp.broadcast_to(ritzv[...], (half, half)), 0.0), axis=1, keepdims=True)
    lam[pl.ds(hrows, half), :] = jnp.broadcast_to(lam_own, (half, W))
    ex[2].start()
    def pass_x(c):
        xown[c].wait_recv()
        xpass[c].start()

    back(3)
    scopy[1].start()
    back(4)

    @pl.when(h == 0)
    def _():
        scopy[1].wait_recv()
        part[4] += inbuf[3]
    for c in bown:
        c.start()
    back(1)
    scopy[0].start()
    back(2)
    pass_x(0)
    pass_x(1)
    shared[1].start()

    @pl.when(h == 0)
    def _():
        scopy[0].wait_recv()
        part[2] += inbuf[1]

    @pl.when(h == 1)
    def _():
        scopy[1].wait_recv()
        part[2] += inbuf[3]

    def pass_products(c):
        bown[c].wait_recv()
        part[2, piece[c]] += inbuf[4, piece[c]]
        bpass[c].start()

    def put_hx(at, v):
        hx[:, at] = v
    times_m(xx.at[0], 0, put_hx)
    pass_x(2)
    pass_x(3)
    shared[2].start()
    times_mt(0)
    pass_products(0)

    def direct(t):
        pl.when(h == 0)(shared[t - 1].wait_recv)
        pl.when(h == 1)(shared[t].wait_recv)
        to_parts(t)
        times_mt(t)

    direct(1)
    pass_products(1)
    pass_products(2)
    for c in xpass[:2]:
        c.wait_recv()
    shared[3].start()
    direct(2)
    pass_products(3)
    for c in xpass[2:]:
        c.wait_recv()
    pl.when(h == 0)(shared[4].start)
    direct(3)
    direct(4)
    loc_p.wait()
    ex[1].wait()
    ex[2].wait()
    @pl.when(h == 1)
    def _():
        scopy[0].wait_recv()
        hx[...] += inbuf[1]
    for c in bpass:
        c.wait_recv()

    loc_rot.wait()
    n = 2 * half
    ct_hi, ct_lo = split(jnp.concatenate(
        [rotv[...], jnp.where(lax.broadcasted_iota(jnp.int32, (n, 3 * n), 1) < n, 0.0, rotv[...])], axis=0))
    ct = jnp.concatenate([ct_hi, ct_lo], axis=0)
    for j in range(L // CH):
        at = slice(j * CH, (j + 1) * CH)
        x = xw[h, :, at]
        res = hx[:, at] + inbuf[2, :, at] - jnp.concatenate([lam[...]] * (CH // W), axis=1) * x
        r_hi, r_lo = split(res)
        p_hi, p_lo = split(pv[:, at])
        b_hi = jnp.concatenate([xx[0, :n, at], r_hi, p_hi], axis=0)
        b_lo = jnp.concatenate([xx[0, n:, at], r_lo, p_lo], axis=0)
        both = mm(ct, b_hi, NN)
        both = both[:2 * n] + both[2 * n:] + mm(ct_hi, b_lo, NN)
        zw[0, :, at] = both[:n]
        hi, lo = split(both[:n])
        zz[:n, at] = hi
        zz[n:, at] = lo
        hi, lo = split(both[n:])
        zzp[:n, at] = hi
        zzp[n:, at] = lo

    def sum_copies(which, g):
        m, c, member, (buf, ssem, rsem) = groups[g]
        return [
            remote(buf.at[which, c], buf.at[which, c], ssem.at[which, k - 1], rsem.at[which, k - 1],
                   member(lax.rem(c + k, m)))
            for k in range(1, m)
        ]

    def sum_start(which, g, value):
        m, c, member, (buf, ssem, rsem) = groups[g]
        buf[which, c] = value
        for copy in sum_copies(which, g):
            copy.start()

    def sum_finish(which, g):
        m, c, member, (buf, ssem, rsem) = groups[g]
        for copy in sum_copies(which, g):
            copy.wait()
        total = buf[which, 0]
        for k in range(1, m):
            total = total + buf[which, k]
        return total

    def z_times_m(t):
        def put(at, v):
            tb[t, :, at] = v
        times_m(zz, t, put)

    def quarters(v):
        return v[:n, :n] + v[:n, n:] + v[n:, :n] + v[n:, n:]

    def s_part(k):
        if k:
            hi, lo = split(zw[k])
            other_z = jnp.concatenate([hi, lo], axis=0)
        else:
            other_z = zz[...]
        hi, lo = split(tb[2 * k])
        return mm(jnp.concatenate([hi, lo], axis=0), other_z, NT)

    def fold(v):
        return jnp.concatenate([v[:half], v[half:]], axis=1)

    def unfold(v):
        return jnp.concatenate([v[:, :n], v[:, n:]], axis=0)

    z_times_m(3)
    tcopy[1].start()
    sum_start(0, 0, fold(quarters(mm(zz[...], zz[...], NT))))
    zcopy.start()
    z_times_m(4)
    tcopy[1].wait_recv()

    @pl.when(h == 0)
    def _():
        tb[4] += tin[1]
    tcopy[2].start()
    z_times_m(1)
    tcopy[0].start()
    sum_start(0, 1, sum_finish(0, 0))
    z_times_m(0)
    z_times_m(2)
    tcopy[0].wait_recv()
    tb[2 * (1 - h)] += tin[0]

    @pl.when(h == 1)
    def _():
        tb[2] += tin[1]
    s = s_part(0)
    zcopy.wait_recv()
    tcopy[2].wait_recv()
    tb[2] += tin[2]
    s = s + s_part(1)
    sum_start(1, 0, fold(quarters(s)))
    a = factor_start(unfold(sum_finish(0, 1)) * (1.0 / ntot))
    a = factor_steps(a, 0, half)
    sum_start(1, 1, sum_finish(1, 0))
    a = factor_steps(a, half, n)
    li = factor_end(a)
    li_hi, li_lo = split(li)
    ll = jnp.concatenate([jnp.concatenate([li_hi, li_hi], axis=1), jnp.concatenate([li_lo, li_lo], axis=1)], axis=0)
    for j in range(L // CH):
        at = slice(j * CH, (j + 1) * CH)
        for k, src in enumerate((zz, zzp)):
            v = mm(ll, src[:, at], NN)
            ostage[k, :, at] = v[:n] + v[n:]
    orows = pl.multiple_of((1 - h) * half, half)
    ocopy = []
    for k, out in enumerate((nc, nd)):
        ocopy.append(remote(ostage.at[k, pl.ds(orows, half)], out.at[:, pl.ds(mine, L)], outs.at[k], outr.at[k], sib))
        ocopy.append(pltpu.make_async_copy(ostage.at[k, pl.ds(hrows, half)], out.at[:, pl.ds(mine, L)], loc_sem.at[2 + k]))
    for c in ocopy:
        c.start()
    s = unfold(sum_finish(1, 1)) * (1.0 / ntot)
    sym = s + jnp.transpose(s)
    v = mm(ll, jnp.concatenate(split(sym), axis=0), NN)
    v = jnp.concatenate(split(v[:n] + v[n:]), axis=0)
    proj[...] = quarters(mm(v, jnp.concatenate([li_hi, li_lo], axis=0), NT))
    for c in ocopy:
        c.wait()
    for c in xown + xpass + shared[1:4] + [zcopy] + scopy + bown + bpass + tcopy:
        c.wait_send()
    pl.when(h == 1)(shared[0].wait_send)
    pl.when(h == 0)(shared[4].wait_send)


def place(*refs):
    for k in range(3):
        refs[3 + k][...] = refs[k][...]


def on_device(dims, ntot, blocks, columns, current, directions, ritz_values, rotation):
    rows_here, slots = columns.shape
    half, length = current.shape
    states = rotation.shape[1]
    total_rows = ntot // W
    any_ = pl.BlockSpec(memory_space=pl.ANY)
    vmem = pl.BlockSpec(memory_space=pltpu.VMEM)
    ga = 2 * dims[-1]
    gb = total_rows // rows_here // dims[-1]
    dma = pltpu.SemaphoreType.DMA
    scratch = [pltpu.VMEM((slots + 1, W, W), F32) for _ in range(RB)] + [
        pltpu.VMEM((L, SLABS * L), BF16),
        pltpu.VMEM((L, SLABS * L), BF16),
        pltpu.VMEM((SLABS + 1, states, L), F32),
        pltpu.VMEM((SLABS, 2 * states, L), BF16),
        pltpu.VMEM((2, states, L), F32),
        pltpu.VMEM((2 * states, L), BF16),
        pltpu.VMEM((2 * states, L), BF16),
        pltpu.VMEM((SLABS, states, L), F32),
        pltpu.VMEM((SLABS, states, L), F32),
        pltpu.VMEM((SLABS, states, L), F32),
        pltpu.VMEM((3, states, L), F32),
        pltpu.VMEM((states, L), F32),
        pltpu.VMEM((states, L), F32),
        pltpu.VMEM((states, W), F32),
        pltpu.VMEM((states, 3 * states), F32),
        pltpu.VMEM((1, half), F32),
        pltpu.VMEM((rows_here, slots), jnp.int32),
        pltpu.VMEM((RB, W), jnp.int32),
        pltpu.SMEM((RB, W), jnp.int32),
        pltpu.VMEM((2, states, L), F32),
        pltpu.VMEM((2, ga, half, 2 * states), F32),
        pltpu.VMEM((2, gb, half, 2 * states), F32),
        dma((RB,)), dma((9,)), dma((3,)), dma((3,)),
        dma((2 * PIECES,)), dma((2 * PIECES,)), dma((SLABS,)), dma((SLABS,)), dma(()), dma(()), dma((3,)), dma((3,)),
        dma((2,)), dma((2,)), dma((2 * PIECES,)), dma((2 * PIECES,)),
        dma((2, ga)), dma((2, ga)), dma((2, gb)), dma((2, gb)), dma((2,)), dma((2,)),
    ]
    outs = pl.pallas_call(
        functools.partial(kernel, dims, ntot),
        out_shape=(
            jax.ShapeDtypeStruct((half, length), F32),
            jax.ShapeDtypeStruct((half, length), F32),
            jax.ShapeDtypeStruct((states, states), F32),
        ),
        in_specs=[any_, any_, any_, any_, any_, any_],
        out_specs=(any_, any_, vmem),
        scratch_shapes=scratch,
        compiler_params=pltpu.CompilerParams(
            collective_id=0, has_side_effects=True, vmem_limit_bytes=58 * 2**20
        ),
        name="lobpcg",
    )(columns, blocks, current, directions, ritz_values.reshape(1, half), rotation.T)
    return pl.pallas_call(
        place,
        out_shape=tuple(jax.ShapeDtypeStruct(o.shape, o.dtype) for o in outs),
        in_specs=[vmem] * 3,
        out_specs=(vmem,) * 3,
        name="place",
    )(*outs)


def solution(mesh):
    rows_n = mesh.shape["row"]
    side = round(rows_n ** (1 / 3))
    dims = (side, side, rows_n // (side * side))
    in_specs = (
        P("row", None, None, None),
        P("row", None),
        P("col", "row"),
        P("col", "row"),
        P("col"),
        P(),
    )
    out_specs = (P("col", "row"), P("col", "row"), P())
    ntot = rows_n * 2 * L
    return jax.shard_map(
        functools.partial(on_device, dims, ntot), mesh=mesh, in_specs=in_specs, out_specs=out_specs, check_vma=False
    )
```

```python
import functools

import jax
import jax.numpy as jnp
from jax import lax
from jax.experimental import pallas as pl
from jax.experimental.pallas import tpu as pltpu
from jax.sharding import PartitionSpec as P

WB = 32
F32 = jnp.float32
BF16 = jnp.bfloat16
MESH = pl.DeviceIdType.MESH
NN = (((1,), (0,)), ((), ()))
NT = (((1,), (1,)), ((), ()))
TN = (((0,), (0,)), ((), ()))

RB = 8
W = 128
L = RB * W
SLABS = WB // RB + 1
CH = 256
PIECES = 4


def mm(a, b, dims):
    return lax.dot_general(a, b, dims, preferred_element_type=F32)


def split(v):
    hi = v.astype(BF16)
    return hi, (v - hi.astype(F32)).astype(BF16)


def factor_start(g):
    n = g.shape[0]
    rows = lax.broadcasted_iota(jnp.int32, (n, 2 * n), 0)
    lanes = lax.broadcasted_iota(jnp.int32, (n, 2 * n), 1)
    a = jnp.concatenate([g, jnp.zeros((n, n), F32)], axis=1) + jnp.where(rows + n == lanes, 1.0, 0.0).astype(F32)
    return [a[8 * i:8 * i + 8] for i in range(n // 8)]


def factor_steps(a, first, last):
    a = list(a)
    sub = lax.broadcasted_iota(jnp.int32, (8, 1), 0)
    for k in range(first, last):
        b, s = divmod(k, 8)
        row = a[b][s:s + 1, :]
        scaled = row * (1.0 / row[:, k:k + 1])
        for i in range(b, len(a)):
            col = a[i][:, k:k + 1]
            if i == b:
                col = jnp.where(sub > s, col, 0.0)
            a[i] = a[i] - col * scaled
    return a


def factor_end(a):
    a = jnp.concatenate(a, axis=0)
    n = a.shape[0]
    rows = lax.broadcasted_iota(jnp.int32, (n, 2 * n), 0)
    lanes = lax.broadcasted_iota(jnp.int32, (n, 2 * n), 1)
    diag = jnp.sum(jnp.where(rows == lanes, a, 0.0), axis=1, keepdims=True)
    return a[:, n:] * (1.0 / jnp.sqrt(diag))


def kernel(dims, ntot, columns, blocks, current, directions, ritz, rot, nc, nd, proj, *scratch):
    stages = scratch[:RB]
    (mh, ml, xw, xx, zw, zz, zzp, part, inbuf, tb, tin, hx, pv, lam, rotv, ritzv, colv, invv, inv_ref, ostage, bufa, bufb,
     blk_sem, loc_sem, exs, exr, xs, xr, cs, cr, zs, zr, ts, tr, ss, sr, bs, br, asa, ara, asb, arb, outs, outr) = scratch[RB:]
    half, full = current.shape
    slots = blocks.shape[1]
    rows_n = 1
    for m in dims:
        rows_n *= m
    r = lax.axis_index("row")
    h = lax.axis_index("col")
    sib = (r, 1 - h)

    ny = dims[-1]
    nb = rows_n // ny
    y = lax.rem(r, ny)
    groups = [
        (2 * ny, 2 * y + h, lambda k: (r - y + k // 2, lax.rem(k, 2)), (bufa, asa, ara)),
        (nb, r // ny, lambda k: (k * ny + y, h), (bufb, asb, arb)),
    ]

    def row_at(k):
        return (lax.rem(r + k + rows_n, rows_n), h)

    barrier = pltpu.get_barrier_semaphore()
    partners = [row_at(k) for k in (-1, 1)]
    for m, c, member, _ in groups:
        for k in range(1, m):
            partners.append(member(lax.rem(c + k, m)))
    for d in partners:
        pl.semaphore_signal(barrier, inc=1, device_id=d, device_id_type=MESH)

    for i in range(RB):
        pltpu.make_async_copy(
            blocks.at[h * RB + i], stages[i].at[pl.ds(0, slots)], blk_sem.at[i]
        ).start()
    mine = pl.multiple_of(h * L, L)
    other = pl.multiple_of((1 - h) * L, L)
    hrows = pl.multiple_of(h * half, half)
    loc_x = [
        pltpu.make_async_copy(current.at[:, pl.ds(w * L, L)], xw.at[w, pl.ds(hrows, half)], loc_sem.at[8 * w])
        for w in range(2)
    ]
    for c in loc_x:
        c.start()
    loc_p = pltpu.make_async_copy(directions.at[:, pl.ds(mine, L)], pv.at[pl.ds(hrows, half)], loc_sem.at[1])
    loc_p.start()
    loc_rot = pltpu.make_async_copy(rot, rotv, loc_sem.at[4])
    loc_rot.start()
    loc_ritz = pltpu.make_async_copy(ritz, ritzv, loc_sem.at[5])
    loc_ritz.start()
    loc_col = pltpu.make_async_copy(columns, colv, loc_sem.at[6])
    loc_col.start()

    for i in range(RB):
        stages[i][slots] = jnp.zeros((W, W), F32)
    zero = jnp.zeros((W, W), BF16)
    for j in range(0, RB, 2):
        for m_ref in (mh, ml):
            m_ref[(j + 1) * W:(j + 2) * W, j * W:(j + 1) * W] = zero
            m_ref[j * W:(j + 1) * W, (WB + j + 1) * W:(WB + j + 2) * W] = zero
    loc_col.wait()
    at = lax.broadcasted_iota(jnp.int32, (RB, slots), 0) + (2 * r + h) * RB
    ahead = colv[pl.ds(pl.multiple_of(h * RB, RB), RB), :] - at
    ahead = jnp.where(ahead < 0, ahead + rows_n * 2 * RB, ahead)
    lanes = lax.broadcasted_iota(jnp.int32, (RB, W), 1)
    found = jnp.full((RB, W), slots, jnp.int32)
    for k in range(slots):
        found = jnp.where(ahead[:, k:k + 1] == lanes, k, found)
    invv[...] = found
    to_smem = pltpu.make_async_copy(invv, inv_ref, loc_sem.at[7])
    to_smem.start()
    to_smem.wait()
    for c in loc_x:
        c.wait()
    pl.semaphore_wait(barrier, len(partners))

    def remote(src, dst, ssem, rsem, dev):
        return pltpu.make_async_remote_copy(
            src_ref=src, dst_ref=dst, send_sem=ssem, recv_sem=rsem, device_id=dev, device_id_type=MESH)

    ex = [
        remote(xw.at[1 - h, pl.ds(hrows, half)], xw.at[1 - h, pl.ds(hrows, half)], exs.at[0], exr.at[0], sib),
        remote(directions.at[:, pl.ds(other, L)], pv.at[pl.ds(hrows, half)], exs.at[1], exr.at[1], sib),
        remote(lam.at[pl.ds(hrows, half)], lam.at[pl.ds(hrows, half)], exs.at[2], exr.at[2], sib),
    ]
    ex[0].start()
    piece = [pl.ds(c * (2 * half // PIECES), 2 * half // PIECES) for c in range(PIECES)]

    def pieces(src, i, dst, j, ssem, rsem, first, dev):
        return [remote(src.at[i, p], dst.at[j, p], ssem.at[first + c], rsem.at[first + c], dev) for c, p in enumerate(piece)]

    def x_piece(c, w):
        return xw.at[w, pl.ds(pl.multiple_of(hrows + c % 2 * (half // 2), half // 2), half // 2)]

    xown = [remote(x_piece(c, c // 2), x_piece(c, c // 2 + 2), xs.at[c], xr.at[c], row_at(-1)) for c in range(PIECES)]
    xpass = [
        remote(x_piece(c, c // 2 + 2), x_piece(c, c // 2 + 4), xs.at[PIECES + c], xr.at[PIECES + c], row_at(-1))
        for c in range(PIECES)
    ]
    shared = [
        remote(xw.at[w, pl.ds(hrows, half)], xw.at[w, pl.ds(hrows, half)], cs.at[w - 1], cr.at[w - 1], sib)
        for w in range(1, SLABS + 1)
    ]
    for c in xown:
        c.start()
    pl.when(h == 1)(shared[0].start)
    ex[1].start()
    zcopy = remote(zw.at[0], zw.at[1], zs, zr, row_at(-1))
    tcopy = [remote(tb.at[t], tin.at[k], ts.at[k], tr.at[k], dev) for k, (t, dev) in enumerate(((1, sib), (3, sib), (4, row_at(1))))]
    scopy = [remote(part.at[t], inbuf.at[t], ss.at[t // 2], sr.at[t // 2], sib) for t in (1, 3)]
    bown = pieces(part, 4, inbuf, 4, bs, br, 0, row_at(1))
    bpass = pieces(part, 2, inbuf, 2, bs, br, PIECES, row_at(1))

    def to_parts(t):
        hi, lo = split(xw[h + t])
        xx[t, :2 * half] = hi
        xx[t, 2 * half:] = lo

    def expand(i):
        pltpu.make_async_copy(
            blocks.at[h * RB + i], stages[i].at[pl.ds(0, slots)], blk_sem.at[i]
        ).wait()
        hi, lo = split(stages[i][0] * 0.5)
        mh[i * W:(i + 1) * W, i * W:(i + 1) * W] = hi
        ml[i * W:(i + 1) * W, i * W:(i + 1) * W] = lo

        def one(d, carry):
            hi, lo = split(stages[i][inv_ref[i, d]])
            at = pl.multiple_of((i + d) * W, W)
            mh[i * W:(i + 1) * W, pl.ds(at, W)] = hi
            ml[i * W:(i + 1) * W, pl.ds(at, W)] = lo
            return carry

        lax.fori_loop(1, WB + 1, one, 0, unroll=4)

    def times_m(src, t, write):
        def chunk(j, lo, hi):
            at = pl.multiple_of(t * L + j * CH, CH)
            a = mm(src[:, lo:hi], mh[lo:hi, pl.ds(at, CH)], NN)
            b = mm(src[:2 * half, lo:hi], ml[lo:hi, pl.ds(at, CH)], NN)
            write(pl.ds(pl.multiple_of(j * CH, CH), CH), a[:2 * half] + a[2 * half:] + b)

        if t == 0 or t == SLABS - 1:
            for j in range(L // CH):
                chunk(j, *((0, (j + 1) * CH) if t == 0 else (j * CH, L)))
        else:
            def body(j, carry):
                chunk(j, 0, L)
                return carry
            lax.fori_loop(0, L // CH, body, 0, unroll=True)

    def times_mt(t):
        def chunk(j, lo, hi):
            at = pl.ds(pl.multiple_of(j * CH, CH), CH)
            a = mm(xx[t, :, lo:hi], mh[at, t * L + lo:t * L + hi], NT)
            b = mm(xx[t, :2 * half, lo:hi], ml[at, t * L + lo:t * L + hi], NT)
            hx[:, at] += a[:2 * half] + a[2 * half:] + b

        if t == 0 or t == SLABS - 1:
            for j in range(L // CH):
                chunk(j, *((j * CH, L) if t == 0 else (0, (j + 1) * CH)))
        else:
            def body(j, carry):
                chunk(j, 0, L)
                return carry
            lax.fori_loop(0, L // CH, body, 0, unroll=True)

    def back(t):
        def put(at, v):
            part[t, :, at] = v
        times_m(xx.at[0], t, put)

    for i in range(RB):
        expand(i)
    ex[0].wait()
    to_parts(0)
    er = lax.broadcasted_iota(jnp.int32, (half, half), 0) == lax.broadcasted_iota(jnp.int32, (half, half), 1)
    loc_ritz.wait()
    lam_own = jnp.sum(jnp.where(er, jnp.broadcast_to(ritzv[...], (half, half)), 0.0), axis=1, keepdims=True)
    lam[pl.ds(hrows, half), :] = jnp.broadcast_to(lam_own, (half, W))
    ex[2].start()
    def pass_x(c):
        xown[c].wait_recv()
        xpass[c].start()

    back(3)
    scopy[1].start()
    back(4)

    @pl.when(h == 0)
    def _():
        scopy[1].wait_recv()
        part[4] += inbuf[3]
    for c in bown:
        c.start()
    back(1)
    scopy[0].start()
    back(2)
    pass_x(0)
    pass_x(1)
    shared[1].start()

    @pl.when(h == 0)
    def _():
        scopy[0].wait_recv()
        part[2] += inbuf[1]

    @pl.when(h == 1)
    def _():
        scopy[1].wait_recv()
        part[2] += inbuf[3]

    def pass_products(c):
        bown[c].wait_recv()
        part[2, piece[c]] += inbuf[4, piece[c]]
        bpass[c].start()

    def put_hx(at, v):
        hx[:, at] = v
    times_m(xx.at[0], 0, put_hx)
    pass_x(2)
    pass_x(3)
    shared[2].start()
    times_mt(0)

    def direct(t):
        pl.when(h == 0)(shared[t - 1].wait_recv)
        pl.when(h == 1)(shared[t].wait_recv)
        to_parts(t)
        times_mt(t)

    direct(1)
    pass_products(0)
    pass_products(1)
    for c in xpass[:2]:
        c.wait_recv()
    shared[3].start()
    direct(2)
    pass_products(2)
    pass_products(3)
    for c in xpass[2:]:
        c.wait_recv()
    pl.when(h == 0)(shared[4].start)
    direct(3)
    direct(4)
    loc_p.wait()
    ex[1].wait()
    ex[2].wait()
    @pl.when(h == 1)
    def _():
        scopy[0].wait_recv()
        hx[...] += inbuf[1]
    for c in bpass:
        c.wait_recv()

    loc_rot.wait()
    n = 2 * half
    ct_hi, ct_lo = split(jnp.concatenate(
        [rotv[...], jnp.where(lax.broadcasted_iota(jnp.int32, (n, 3 * n), 1) < n, 0.0, rotv[...])], axis=0))
    ct = jnp.concatenate([ct_hi, ct_lo], axis=0)
    for j in range(L // CH):
        at = slice(j * CH, (j + 1) * CH)
        x = xw[h, :, at]
        res = hx[:, at] + inbuf[2, :, at] - jnp.concatenate([lam[...]] * (CH // W), axis=1) * x
        r_hi, r_lo = split(res)
        p_hi, p_lo = split(pv[:, at])
        b_hi = jnp.concatenate([xx[0, :n, at], r_hi, p_hi], axis=0)
        b_lo = jnp.concatenate([xx[0, n:, at], r_lo, p_lo], axis=0)
        both = mm(ct, b_hi, NN)
        both = both[:2 * n] + both[2 * n:] + mm(ct_hi, b_lo, NN)
        zw[0, :, at] = both[:n]
        hi, lo = split(both[:n])
        zz[:n, at] = hi
        zz[n:, at] = lo
        hi, lo = split(both[n:])
        zzp[:n, at] = hi
        zzp[n:, at] = lo

    def sum_copies(which, g):
        m, c, member, (buf, ssem, rsem) = groups[g]
        return [
            remote(buf.at[which, c], buf.at[which, c], ssem.at[which, k - 1], rsem.at[which, k - 1],
                   member(lax.rem(c + k, m)))
            for k in range(1, m)
        ]

    def sum_start(which, g, value):
        m, c, member, (buf, ssem, rsem) = groups[g]
        buf[which, c] = value
        for copy in sum_copies(which, g):
            copy.start()

    def sum_finish(which, g):
        m, c, member, (buf, ssem, rsem) = groups[g]
        for copy in sum_copies(which, g):
            copy.wait()
        total = buf[which, 0]
        for k in range(1, m):
            total = total + buf[which, k]
        return total

    def z_times_m(t):
        def put(at, v):
            tb[t, :, at] = v
        times_m(zz, t, put)

    def quarters(v):
        return v[:n, :n] + v[:n, n:] + v[n:, :n] + v[n:, n:]

    def s_part(k):
        if k:
            hi, lo = split(zw[k])
            other_z = jnp.concatenate([hi, lo], axis=0)
        else:
            other_z = zz[...]
        hi, lo = split(tb[2 * k])
        return mm(jnp.concatenate([hi, lo], axis=0), other_z, NT)

    def fold(v):
        return jnp.concatenate([v[:half], v[half:]], axis=1)

    def unfold(v):
        return jnp.concatenate([v[:, :n], v[:, n:]], axis=0)

    z_times_m(3)
    tcopy[1].start()
    sum_start(0, 0, fold(quarters(mm(zz[...], zz[...], NT))))
    zcopy.start()
    z_times_m(4)
    tcopy[1].wait_recv()

    @pl.when(h == 0)
    def _():
        tb[4] += tin[1]
    tcopy[2].start()
    z_times_m(1)
    tcopy[0].start()
    sum_start(0, 1, sum_finish(0, 0))
    z_times_m(0)
    z_times_m(2)
    tcopy[0].wait_recv()
    tb[2 * (1 - h)] += tin[0]

    @pl.when(h == 1)
    def _():
        tb[2] += tin[1]
    s = s_part(0)
    zcopy.wait_recv()
    tcopy[2].wait_recv()
    tb[2] += tin[2]
    s = s + s_part(1)
    sum_start(1, 0, fold(quarters(s)))
    sum_start(1, 1, sum_finish(1, 0))
    a = factor_start(unfold(sum_finish(0, 1)) * (1.0 / ntot))
    a = factor_steps(a, 0, n)
    li = factor_end(a)
    li_hi, li_lo = split(li)
    ll = jnp.concatenate([jnp.concatenate([li_hi, li_hi], axis=1), jnp.concatenate([li_lo, li_lo], axis=1)], axis=0)
    for j in range(L // CH):
        at = slice(j * CH, (j + 1) * CH)
        for k, src in enumerate((zz, zzp)):
            v = mm(ll, src[:, at], NN)
            ostage[k, :, at] = v[:n] + v[n:]
    orows = pl.multiple_of((1 - h) * half, half)
    ocopy = []
    for k, out in enumerate((nc, nd)):
        ocopy.append(remote(ostage.at[k, pl.ds(orows, half)], out.at[:, pl.ds(mine, L)], outs.at[k], outr.at[k], sib))
        ocopy.append(pltpu.make_async_copy(ostage.at[k, pl.ds(hrows, half)], out.at[:, pl.ds(mine, L)], loc_sem.at[2 + k]))
    for c in ocopy:
        c.start()
    s = unfold(sum_finish(1, 1)) * (1.0 / ntot)
    sym = s + jnp.transpose(s)
    v = mm(ll, jnp.concatenate(split(sym), axis=0), NN)
    v = jnp.concatenate(split(v[:n] + v[n:]), axis=0)
    proj[...] = quarters(mm(v, jnp.concatenate([li_hi, li_lo], axis=0), NT))
    for c in ocopy:
        c.wait()
    for c in xown + xpass + shared[1:4] + [zcopy] + scopy + bown + bpass + tcopy:
        c.wait_send()
    pl.when(h == 1)(shared[0].wait_send)
    pl.when(h == 0)(shared[4].wait_send)


def place(*refs):
    for k in range(3):
        refs[3 + k][...] = refs[k][...]


def on_device(dims, ntot, blocks, columns, current, directions, ritz_values, rotation):
    rows_here, slots = columns.shape
    half, length = current.shape
    states = rotation.shape[1]
    total_rows = ntot // W
    any_ = pl.BlockSpec(memory_space=pl.ANY)
    vmem = pl.BlockSpec(memory_space=pltpu.VMEM)
    ga = 2 * dims[-1]
    gb = total_rows // rows_here // dims[-1]
    dma = pltpu.SemaphoreType.DMA
    scratch = [pltpu.VMEM((slots + 1, W, W), F32) for _ in range(RB)] + [
        pltpu.VMEM((L, SLABS * L), BF16),
        pltpu.VMEM((L, SLABS * L), BF16),
        pltpu.VMEM((SLABS + 1, states, L), F32),
        pltpu.VMEM((SLABS, 2 * states, L), BF16),
        pltpu.VMEM((2, states, L), F32),
        pltpu.VMEM((2 * states, L), BF16),
        pltpu.VMEM((2 * states, L), BF16),
        pltpu.VMEM((SLABS, states, L), F32),
        pltpu.VMEM((SLABS, states, L), F32),
        pltpu.VMEM((SLABS, states, L), F32),
        pltpu.VMEM((3, states, L), F32),
        pltpu.VMEM((states, L), F32),
        pltpu.VMEM((states, L), F32),
        pltpu.VMEM((states, W), F32),
        pltpu.VMEM((states, 3 * states), F32),
        pltpu.VMEM((1, half), F32),
        pltpu.VMEM((rows_here, slots), jnp.int32),
        pltpu.VMEM((RB, W), jnp.int32),
        pltpu.SMEM((RB, W), jnp.int32),
        pltpu.VMEM((2, states, L), F32),
        pltpu.VMEM((2, ga, half, 2 * states), F32),
        pltpu.VMEM((2, gb, half, 2 * states), F32),
        dma((RB,)), dma((9,)), dma((3,)), dma((3,)),
        dma((2 * PIECES,)), dma((2 * PIECES,)), dma((SLABS,)), dma((SLABS,)), dma(()), dma(()), dma((3,)), dma((3,)),
        dma((2,)), dma((2,)), dma((2 * PIECES,)), dma((2 * PIECES,)),
        dma((2, ga)), dma((2, ga)), dma((2, gb)), dma((2, gb)), dma((2,)), dma((2,)),
    ]
    outs = pl.pallas_call(
        functools.partial(kernel, dims, ntot),
        out_shape=(
            jax.ShapeDtypeStruct((half, length), F32),
            jax.ShapeDtypeStruct((half, length), F32),
            jax.ShapeDtypeStruct((states, states), F32),
        ),
        in_specs=[any_, any_, any_, any_, any_, any_],
        out_specs=(any_, any_, vmem),
        scratch_shapes=scratch,
        compiler_params=pltpu.CompilerParams(
            collective_id=0, has_side_effects=True, vmem_limit_bytes=58 * 2**20
        ),
        name="lobpcg",
    )(columns, blocks, current, directions, ritz_values.reshape(1, half), rotation.T)
    return pl.pallas_call(
        place,
        out_shape=tuple(jax.ShapeDtypeStruct(o.shape, o.dtype) for o in outs),
        in_specs=[vmem] * 3,
        out_specs=(vmem,) * 3,
        name="place",
    )(*outs)


def solution(mesh):
    rows_n = mesh.shape["row"]
    side = round(rows_n ** (1 / 3))
    dims = (side, side, rows_n // (side * side))
    in_specs = (
        P("row", None, None, None),
        P("row", None),
        P("col", "row"),
        P("col", "row"),
        P("col"),
        P(),
    )
    out_specs = (P("col", "row"), P("col", "row"), P())
    ntot = rows_n * 2 * L
    return jax.shard_map(
        functools.partial(on_device, dims, ntot), mesh=mesh, in_specs=in_specs, out_specs=out_specs, check_vma=False
    )
```

```python
import functools

import jax
import jax.numpy as jnp
from jax import lax
from jax.experimental import pallas as pl
from jax.experimental.pallas import tpu as pltpu
from jax.sharding import PartitionSpec as P

WB = 32
F32 = jnp.float32
BF16 = jnp.bfloat16
MESH = pl.DeviceIdType.MESH
NN = (((1,), (0,)), ((), ()))
NT = (((1,), (1,)), ((), ()))
TN = (((0,), (0,)), ((), ()))

RB = 8
W = 128
L = RB * W
SLABS = WB // RB + 1
CH = 256
PIECES = 4


def mm(a, b, dims):
    return lax.dot_general(a, b, dims, preferred_element_type=F32)


def split(v):
    hi = v.astype(BF16)
    return hi, (v - hi.astype(F32)).astype(BF16)


def factor_start(g):
    n = g.shape[0]
    rows = lax.broadcasted_iota(jnp.int32, (n, 2 * n), 0)
    lanes = lax.broadcasted_iota(jnp.int32, (n, 2 * n), 1)
    a = jnp.concatenate([g, jnp.zeros((n, n), F32)], axis=1) + jnp.where(rows + n == lanes, 1.0, 0.0).astype(F32)
    return [a[8 * i:8 * i + 8] for i in range(n // 8)]


def factor_steps(a, first, last):
    a = list(a)
    sub = lax.broadcasted_iota(jnp.int32, (8, 1), 0)
    for k in range(first, last):
        b, s = divmod(k, 8)
        row = a[b][s:s + 1, :]
        scaled = row * (1.0 / row[:, k:k + 1])
        for i in range(b, len(a)):
            col = a[i][:, k:k + 1]
            if i == b:
                col = jnp.where(sub > s, col, 0.0)
            a[i] = a[i] - col * scaled
    return a


def factor_end(a):
    a = jnp.concatenate(a, axis=0)
    n = a.shape[0]
    rows = lax.broadcasted_iota(jnp.int32, (n, 2 * n), 0)
    lanes = lax.broadcasted_iota(jnp.int32, (n, 2 * n), 1)
    diag = jnp.sum(jnp.where(rows == lanes, a, 0.0), axis=1, keepdims=True)
    return a[:, n:] * (1.0 / jnp.sqrt(diag))


def kernel(dims, ntot, columns, blocks, current, directions, ritz, rot, nc, nd, proj, *scratch):
    stages = scratch[:RB]
    (mh, ml, xw, xx, zw, zz, zzp, part, inbuf, tb, tin, hx, hxt, pv, lam, rotv, ritzv, colv, invv, inv_ref, ostage, bufa, bufb,
     blk_sem, loc_sem, exs, exr, xs, xr, cs, cr, zs, zr, ts, tr, ss, sr, bs, br, asa, ara, asb, arb, outs, outr) = scratch[RB:]
    half, full = current.shape
    slots = blocks.shape[1]
    rows_n = 1
    for m in dims:
        rows_n *= m
    r = lax.axis_index("row")
    h = lax.axis_index("col")
    sib = (r, 1 - h)

    ny = dims[-1]
    nb = rows_n // ny
    y = lax.rem(r, ny)
    groups = [
        (2 * ny, 2 * y + h, lambda k: (r - y + k // 2, lax.rem(k, 2)), (bufa, asa, ara)),
        (nb, r // ny, lambda k: (k * ny + y, h), (bufb, asb, arb)),
    ]

    def row_at(k):
        return (lax.rem(r + k + rows_n, rows_n), h)

    barrier = pltpu.get_barrier_semaphore()
    partners = [row_at(k) for k in (-1, 1)]
    for m, c, member, _ in groups:
        for k in range(1, m):
            partners.append(member(lax.rem(c + k, m)))
    for d in partners:
        pl.semaphore_signal(barrier, inc=1, device_id=d, device_id_type=MESH)

    for i in range(RB):
        pltpu.make_async_copy(
            blocks.at[h * RB + i], stages[i].at[pl.ds(0, slots)], blk_sem.at[i]
        ).start()
    mine = pl.multiple_of(h * L, L)
    other = pl.multiple_of((1 - h) * L, L)
    hrows = pl.multiple_of(h * half, half)
    loc_x = [
        pltpu.make_async_copy(current.at[:, pl.ds(w * L, L)], xw.at[w, pl.ds(hrows, half)], loc_sem.at[8 * w])
        for w in range(2)
    ]
    for c in loc_x:
        c.start()
    loc_p = pltpu.make_async_copy(directions.at[:, pl.ds(mine, L)], pv.at[pl.ds(hrows, half)], loc_sem.at[1])
    loc_p.start()
    loc_rot = pltpu.make_async_copy(rot, rotv, loc_sem.at[4])
    loc_rot.start()
    loc_ritz = pltpu.make_async_copy(ritz, ritzv, loc_sem.at[5])
    loc_ritz.start()
    loc_col = pltpu.make_async_copy(columns, colv, loc_sem.at[6])
    loc_col.start()

    for i in range(RB):
        stages[i][slots] = jnp.zeros((W, W), F32)
    zero = jnp.zeros((W, W), BF16)
    for j in range(0, RB, 2):
        for m_ref in (mh, ml):
            m_ref[(j + 1) * W:(j + 2) * W, j * W:(j + 1) * W] = zero
            m_ref[j * W:(j + 1) * W, (WB + j + 1) * W:(WB + j + 2) * W] = zero
    loc_col.wait()
    at = lax.broadcasted_iota(jnp.int32, (RB, slots), 0) + (2 * r + h) * RB
    ahead = colv[pl.ds(pl.multiple_of(h * RB, RB), RB), :] - at
    ahead = jnp.where(ahead < 0, ahead + rows_n * 2 * RB, ahead)
    lanes = lax.broadcasted_iota(jnp.int32, (RB, W), 1)
    found = jnp.full((RB, W), slots, jnp.int32)
    for k in range(slots):
        found = jnp.where(ahead[:, k:k + 1] == lanes, k, found)
    invv[...] = found
    to_smem = pltpu.make_async_copy(invv, inv_ref, loc_sem.at[7])
    to_smem.start()
    to_smem.wait()
    for c in loc_x:
        c.wait()
    pl.semaphore_wait(barrier, len(partners))

    def remote(src, dst, ssem, rsem, dev):
        return pltpu.make_async_remote_copy(
            src_ref=src, dst_ref=dst, send_sem=ssem, recv_sem=rsem, device_id=dev, device_id_type=MESH)

    ex = [
        remote(xw.at[1 - h, pl.ds(hrows, half)], xw.at[1 - h, pl.ds(hrows, half)], exs.at[0], exr.at[0], sib),
        remote(directions.at[:, pl.ds(other, L)], pv.at[pl.ds(hrows, half)], exs.at[1], exr.at[1], sib),
        remote(lam.at[pl.ds(hrows, half)], lam.at[pl.ds(hrows, half)], exs.at[2], exr.at[2], sib),
    ]
    ex[0].start()
    piece = [pl.ds(c * (2 * half // PIECES), 2 * half // PIECES) for c in range(PIECES)]

    def pieces(src, i, dst, j, ssem, rsem, first, dev):
        return [remote(src.at[i, p], dst.at[j, p], ssem.at[first + c], rsem.at[first + c], dev) for c, p in enumerate(piece)]

    def x_piece(c, w):
        return xw.at[w, pl.ds(pl.multiple_of(hrows + c % 2 * (half // 2), half // 2), half // 2)]

    xown = [remote(x_piece(c, c // 2), x_piece(c, c // 2 + 2), xs.at[c], xr.at[c], row_at(-1)) for c in range(PIECES)]
    xpass = [
        remote(x_piece(c, c // 2 + 2), x_piece(c, c // 2 + 4), xs.at[PIECES + c], xr.at[PIECES + c], row_at(-1))
        for c in range(PIECES)
    ]
    shared = [
        remote(xw.at[w, pl.ds(hrows, half)], xw.at[w, pl.ds(hrows, half)], cs.at[w - 1], cr.at[w - 1], sib)
        for w in range(1, SLABS + 1)
    ]
    for c in xown:
        c.start()
    pl.when(h == 1)(shared[0].start)
    ex[1].start()
    zcopy = remote(zw.at[0], zw.at[1], zs, zr, row_at(-1))
    tcopy = [remote(tb.at[t], tin.at[k], ts.at[k], tr.at[k], dev) for k, (t, dev) in enumerate(((1, sib), (3, sib), (4, row_at(1))))]
    scopy = [remote(part.at[t], inbuf.at[t], ss.at[t // 2], sr.at[t // 2], sib) for t in (1, 3)]
    bown = pieces(part, 4, inbuf, 4, bs, br, 0, row_at(1))
    bpass = pieces(part, 2, inbuf, 2, bs, br, PIECES, row_at(1))

    def to_parts(t):
        hi, lo = split(xw[h + t])
        xx[t, :2 * half] = hi
        xx[t, 2 * half:] = lo

    def expand(i):
        pltpu.make_async_copy(
            blocks.at[h * RB + i], stages[i].at[pl.ds(0, slots)], blk_sem.at[i]
        ).wait()
        hi, lo = split(stages[i][0] * 0.5)
        mh[i * W:(i + 1) * W, i * W:(i + 1) * W] = hi
        ml[i * W:(i + 1) * W, i * W:(i + 1) * W] = lo

        def one(d, carry):
            hi, lo = split(stages[i][inv_ref[i, d]])
            at = pl.multiple_of((i + d) * W, W)
            mh[i * W:(i + 1) * W, pl.ds(at, W)] = hi
            ml[i * W:(i + 1) * W, pl.ds(at, W)] = lo
            return carry

        lax.fori_loop(1, WB + 1, one, 0, unroll=4)

    def times_m(src, t, write):
        def chunk(j, lo, hi):
            at = pl.multiple_of(t * L + j * CH, CH)
            a = mm(src[:, lo:hi], mh[lo:hi, pl.ds(at, CH)], NN)
            b = mm(src[:2 * half, lo:hi], ml[lo:hi, pl.ds(at, CH)], NN)
            write(pl.ds(pl.multiple_of(j * CH, CH), CH), a[:2 * half] + a[2 * half:] + b)

        if t == 0 or t == SLABS - 1:
            for j in range(L // CH):
                chunk(j, *((0, (j + 1) * CH) if t == 0 else (j * CH, L)))
        else:
            def body(j, carry):
                chunk(j, 0, L)
                return carry
            lax.fori_loop(0, L // CH, body, 0, unroll=True)

    def times_mt(t):
        def chunk(j, lo, hi):
            at = pl.ds(pl.multiple_of(j * CH, CH), CH)
            v = mm(mh[at, t * L + lo:t * L + hi], xx[t, :, lo:hi], NT)
            v = v + mm(ml[at, t * L + lo:t * L + hi], xx[t, :, lo:hi], NT)
            hxt[at, :] = v if t == 0 else hxt[at, :] + v

        if t == 0 or t == SLABS - 1:
            for j in range(L // CH):
                chunk(j, *((j * CH, L) if t == 0 else (0, (j + 1) * CH)))
        else:
            def body(j, carry):
                chunk(j, 0, L)
                return carry
            lax.fori_loop(0, L // CH, body, 0, unroll=True)

    def back(t):
        def put(at, v):
            part[t, :, at] = v
        times_m(xx.at[0], t, put)

    for i in range(RB):
        expand(i)
    ex[0].wait()
    to_parts(0)
    er = lax.broadcasted_iota(jnp.int32, (half, half), 0) == lax.broadcasted_iota(jnp.int32, (half, half), 1)
    loc_ritz.wait()
    lam_own = jnp.sum(jnp.where(er, jnp.broadcast_to(ritzv[...], (half, half)), 0.0), axis=1, keepdims=True)
    lam[pl.ds(hrows, half), :] = jnp.broadcast_to(lam_own, (half, W))
    ex[2].start()
    def pass_x(c):
        xown[c].wait_recv()
        xpass[c].start()

    back(3)
    scopy[1].start()
    back(4)

    @pl.when(h == 0)
    def _():
        scopy[1].wait_recv()
        part[4] += inbuf[3]
    for c in bown:
        c.start()
    back(1)
    scopy[0].start()
    back(2)
    pass_x(0)
    pass_x(1)
    shared[1].start()

    @pl.when(h == 0)
    def _():
        scopy[0].wait_recv()
        part[2] += inbuf[1]

    @pl.when(h == 1)
    def _():
        scopy[1].wait_recv()
        part[2] += inbuf[3]

    def pass_products(c):
        bown[c].wait_recv()
        part[2, piece[c]] += inbuf[4, piece[c]]
        bpass[c].start()

    def put_hx(at, v):
        hx[:, at] = v
    times_m(xx.at[0], 0, put_hx)
    pass_x(2)
    pass_x(3)
    shared[2].start()
    times_mt(0)

    def direct(t):
        pl.when(h == 0)(shared[t - 1].wait_recv)
        pl.when(h == 1)(shared[t].wait_recv)
        to_parts(t)
        times_mt(t)

    direct(1)
    pass_products(0)
    pass_products(1)
    for c in xpass[:2]:
        c.wait_recv()
    shared[3].start()
    direct(2)
    pass_products(2)
    pass_products(3)
    for c in xpass[2:]:
        c.wait_recv()
    pl.when(h == 0)(shared[4].start)
    direct(3)
    direct(4)
    loc_p.wait()
    ex[1].wait()
    ex[2].wait()
    @pl.when(h == 1)
    def _():
        scopy[0].wait_recv()
        hx[...] += inbuf[1]
    for c in bpass:
        c.wait_recv()

    loc_rot.wait()
    n = 2 * half
    ct_hi, ct_lo = split(jnp.concatenate(
        [rotv[...], jnp.where(lax.broadcasted_iota(jnp.int32, (n, 3 * n), 1) < n, 0.0, rotv[...])], axis=0))
    ct = jnp.concatenate([ct_hi, ct_lo], axis=0)
    for j in range(L // CH):
        at = slice(j * CH, (j + 1) * CH)
        x = xw[h, :, at]
        cols = jnp.transpose(hxt[at, :])
        res = cols[:n] + cols[n:] + hx[:, at] + inbuf[2, :, at] - jnp.concatenate([lam[...]] * (CH // W), axis=1) * x
        r_hi, r_lo = split(res)
        p_hi, p_lo = split(pv[:, at])
        b_hi = jnp.concatenate([xx[0, :n, at], r_hi, p_hi], axis=0)
        b_lo = jnp.concatenate([xx[0, n:, at], r_lo, p_lo], axis=0)
        both = mm(ct, b_hi, NN)
        both = both[:2 * n] + both[2 * n:] + mm(ct_hi, b_lo, NN)
        zw[0, :, at] = both[:n]
        hi, lo = split(both[:n])
        zz[:n, at] = hi
        zz[n:, at] = lo
        hi, lo = split(both[n:])
        zzp[:n, at] = hi
        zzp[n:, at] = lo

    def sum_copies(which, g):
        m, c, member, (buf, ssem, rsem) = groups[g]
        return [
            remote(buf.at[which, c], buf.at[which, c], ssem.at[which, k - 1], rsem.at[which, k - 1],
                   member(lax.rem(c + k, m)))
            for k in range(1, m)
        ]

    def sum_start(which, g, value):
        m, c, member, (buf, ssem, rsem) = groups[g]
        buf[which, c] = value
        for copy in sum_copies(which, g):
            copy.start()

    def sum_finish(which, g):
        m, c, member, (buf, ssem, rsem) = groups[g]
        for copy in sum_copies(which, g):
            copy.wait()
        total = buf[which, 0]
        for k in range(1, m):
            total = total + buf[which, k]
        return total

    def z_times_m(t):
        def put(at, v):
            tb[t, :, at] = v
        times_m(zz, t, put)

    def quarters(v):
        return v[:n, :n] + v[:n, n:] + v[n:, :n] + v[n:, n:]

    def s_part(k):
        if k:
            hi, lo = split(zw[k])
            other_z = jnp.concatenate([hi, lo], axis=0)
        else:
            other_z = zz[...]
        hi, lo = split(tb[2 * k])
        return mm(jnp.concatenate([hi, lo], axis=0), other_z, NT)

    def fold(v):
        return jnp.concatenate([v[:half], v[half:]], axis=1)

    def unfold(v):
        return jnp.concatenate([v[:, :n], v[:, n:]], axis=0)

    z_times_m(3)
    tcopy[1].start()
    sum_start(0, 0, fold(quarters(mm(zz[...], zz[...], NT))))
    zcopy.start()
    z_times_m(4)
    tcopy[1].wait_recv()

    @pl.when(h == 0)
    def _():
        tb[4] += tin[1]
    tcopy[2].start()
    z_times_m(1)
    tcopy[0].start()
    sum_start(0, 1, sum_finish(0, 0))
    z_times_m(0)
    z_times_m(2)
    tcopy[0].wait_recv()
    tb[2 * (1 - h)] += tin[0]

    @pl.when(h == 1)
    def _():
        tb[2] += tin[1]
    s = s_part(0)
    zcopy.wait_recv()
    tcopy[2].wait_recv()
    tb[2] += tin[2]
    s = s + s_part(1)
    sum_start(1, 0, fold(quarters(s)))
    sum_start(1, 1, sum_finish(1, 0))
    a = factor_start(unfold(sum_finish(0, 1)) * (1.0 / ntot))
    a = factor_steps(a, 0, n)
    li = factor_end(a)
    li_hi, li_lo = split(li)
    ll = jnp.concatenate([jnp.concatenate([li_hi, li_hi], axis=1), jnp.concatenate([li_lo, li_lo], axis=1)], axis=0)
    for j in range(L // CH):
        at = slice(j * CH, (j + 1) * CH)
        for k, src in enumerate((zz, zzp)):
            v = mm(ll, src[:, at], NN)
            ostage[k, :, at] = v[:n] + v[n:]
    orows = pl.multiple_of((1 - h) * half, half)
    ocopy = []
    for k, out in enumerate((nc, nd)):
        ocopy.append(remote(ostage.at[k, pl.ds(orows, half)], out.at[:, pl.ds(mine, L)], outs.at[k], outr.at[k], sib))
        ocopy.append(pltpu.make_async_copy(ostage.at[k, pl.ds(hrows, half)], out.at[:, pl.ds(mine, L)], loc_sem.at[2 + k]))
    for c in ocopy:
        c.start()
    s = unfold(sum_finish(1, 1)) * (1.0 / ntot)
    sym = s + jnp.transpose(s)
    v = mm(ll, jnp.concatenate(split(sym), axis=0), NN)
    v = jnp.concatenate(split(v[:n] + v[n:]), axis=0)
    proj[...] = quarters(mm(v, jnp.concatenate([li_hi, li_lo], axis=0), NT))
    for c in ocopy:
        c.wait()
    for c in xown + xpass + shared[1:4] + [zcopy] + scopy + bown + bpass + tcopy:
        c.wait_send()
    pl.when(h == 1)(shared[0].wait_send)
    pl.when(h == 0)(shared[4].wait_send)


def place(*refs):
    for k in range(3):
        refs[3 + k][...] = refs[k][...]


def on_device(dims, ntot, blocks, columns, current, directions, ritz_values, rotation):
    rows_here, slots = columns.shape
    half, length = current.shape
    states = rotation.shape[1]
    total_rows = ntot // W
    any_ = pl.BlockSpec(memory_space=pl.ANY)
    vmem = pl.BlockSpec(memory_space=pltpu.VMEM)
    ga = 2 * dims[-1]
    gb = total_rows // rows_here // dims[-1]
    dma = pltpu.SemaphoreType.DMA
    scratch = [pltpu.VMEM((slots + 1, W, W), F32) for _ in range(RB)] + [
        pltpu.VMEM((L, SLABS * L), BF16),
        pltpu.VMEM((L, SLABS * L), BF16),
        pltpu.VMEM((SLABS + 1, states, L), F32),
        pltpu.VMEM((SLABS, 2 * states, L), BF16),
        pltpu.VMEM((2, states, L), F32),
        pltpu.VMEM((2 * states, L), BF16),
        pltpu.VMEM((2 * states, L), BF16),
        pltpu.VMEM((SLABS, states, L), F32),
        pltpu.VMEM((SLABS, states, L), F32),
        pltpu.VMEM((SLABS, states, L), F32),
        pltpu.VMEM((3, states, L), F32),
        pltpu.VMEM((states, L), F32),
        pltpu.VMEM((L, 2 * states), F32),
        pltpu.VMEM((states, L), F32),
        pltpu.VMEM((states, W), F32),
        pltpu.VMEM((states, 3 * states), F32),
        pltpu.VMEM((1, half), F32),
        pltpu.VMEM((rows_here, slots), jnp.int32),
        pltpu.VMEM((RB, W), jnp.int32),
        pltpu.SMEM((RB, W), jnp.int32),
        pltpu.VMEM((2, states, L), F32),
        pltpu.VMEM((2, ga, half, 2 * states), F32),
        pltpu.VMEM((2, gb, half, 2 * states), F32),
        dma((RB,)), dma((9,)), dma((3,)), dma((3,)),
        dma((2 * PIECES,)), dma((2 * PIECES,)), dma((SLABS,)), dma((SLABS,)), dma(()), dma(()), dma((3,)), dma((3,)),
        dma((2,)), dma((2,)), dma((2 * PIECES,)), dma((2 * PIECES,)),
        dma((2, ga)), dma((2, ga)), dma((2, gb)), dma((2, gb)), dma((2,)), dma((2,)),
    ]
    outs = pl.pallas_call(
        functools.partial(kernel, dims, ntot),
        out_shape=(
            jax.ShapeDtypeStruct((half, length), F32),
            jax.ShapeDtypeStruct((half, length), F32),
            jax.ShapeDtypeStruct((states, states), F32),
        ),
        in_specs=[any_, any_, any_, any_, any_, any_],
        out_specs=(any_, any_, vmem),
        scratch_shapes=scratch,
        compiler_params=pltpu.CompilerParams(
            collective_id=0, has_side_effects=True, vmem_limit_bytes=58 * 2**20
        ),
        name="lobpcg",
    )(columns, blocks, current, directions, ritz_values.reshape(1, half), rotation.T)
    return pl.pallas_call(
        place,
        out_shape=tuple(jax.ShapeDtypeStruct(o.shape, o.dtype) for o in outs),
        in_specs=[vmem] * 3,
        out_specs=(vmem,) * 3,
        name="place",
    )(*outs)


def solution(mesh):
    rows_n = mesh.shape["row"]
    side = round(rows_n ** (1 / 3))
    dims = (side, side, rows_n // (side * side))
    in_specs = (
        P("row", None, None, None),
        P("row", None),
        P("col", "row"),
        P("col", "row"),
        P("col"),
        P(),
    )
    out_specs = (P("col", "row"), P("col", "row"), P())
    ntot = rows_n * 2 * L
    return jax.shard_map(
        functools.partial(on_device, dims, ntot), mesh=mesh, in_specs=in_specs, out_specs=out_specs, check_vma=False
    )
```
